32 devices in a mesh: groups: 2 (over y), blk: 4 (over z), basis: 2 (over x), col: 2 (over core).
Axes of the slice: x: 2, y: 2, z: 4, core: 2. Of those that a mesh axis runs over, the one named last changes fastest.
Arguments:
- right_panel: float32 [256, 256, 64], P(('groups', 'blk'), None, 'col'), parts along dimension 0, may hold values from -6 to 6
- near_field_blocks: bfloat16 [1024, 256, 256], P(('groups', 'blk'), 'basis'), parts along dimension 0, may hold values from -0.1875 to 0.1875
- near_list: int32 [1024, 2], P(('groups', 'blk')), parts along dimension 0, may hold values from 0 to 127, as said below
- cluster_basis: bfloat16 [256, 256, 64], P(('groups', 'blk'), 'basis'), parts along dimension 0, may hold values from -0.375 to 0.375
- coupling: bfloat16 [1024, 64, 64], P(('groups', 'blk')), parts along dimension 0, may hold values from -0.375 to 0.375
- far_list: int32 [1024, 2], P(('groups', 'blk')), parts along dimension 0, may hold values from 0 to 127, as said below
Outputs:
- krylov_one: float32 [256, 256, 64], P(('groups', 'blk'), 'basis', 'col'), parts along dimension 0
- krylov_two: float32 [256, 256, 64], P(('groups', 'blk'), 'basis', 'col'), parts along dimension 0
The draws below stay inside these ranges and needn't reach their ends.
There are 2 independent parts, one for each index of `groups`. The reference program is written for one: setup_inputs(seed, part) draws one part's arguments, and reference() takes and returns one part's arrays. A program takes and returns all parts, laid end to end along the dimension named above; each array names one. Nothing has to cross between parts.
Inputs may be any that keep to these rules, and one draw needn't show every extreme that they name: `near_list`: entry t names a row cluster held by blk index b = t // 128, that is within [b * 32, (b + 1) * 32), and a column cluster held by index b - 1, b or b + 1 of blk taken around the loop of all blk indices (4 here); every index has entries of all three kinds. Clusters may repeat. `far_list`: entry p names a row cluster held by blk index p // 128 and any column cluster. Pairs may repeat.
All inputs are finite; a program needn't handle non-finite values.
Results may differ from the reference program's by a relative error of at most 0.0053.
Values may be sent and summed in bfloat16 or wider, within the bound.
No kernel may reach another device: no remote copies, remote signals or barrier semaphores. Data moves between devices by JAX's collectives and lax.ppermute only.
A program may use at most 64 MiB of HBM per device.

```python
import jax
import jax.numpy as jnp
from jax import lax

LEAF = 256
RANK = 64
COLS = 64
CL = 32
NB_DEV = 128
NF_DEV = 128
NCL = 128
NB_TOT = 512
NF_TOT = 512


def draw_near_list(key, part):
    key = jax.random.fold_in(key, 11)
    key_rows, key_shift, key_cols = jax.random.split(key, 3)
    cycle_size = NB_TOT // NB_DEV
    entries = jnp.arange(NB_TOT, dtype=jnp.int32)
    device = entries // NB_DEV
    row_ids = device * CL + jax.random.randint(key_rows, (NB_TOT,), 0, CL, dtype=jnp.int32)
    position = entries % NB_DEV
    random_offset = jax.random.randint(key_shift, (NB_TOT,), -1, 2, dtype=jnp.int32)
    offset = jnp.where(position < 3, position - 1, random_offset)
    column = (device + offset + cycle_size) % cycle_size * CL + jax.random.randint(key_cols, (NB_TOT,), 0, CL, dtype=jnp.int32)
    return jnp.stack([row_ids, column], 1).astype(jnp.int32)


def draw_far_list(key, part):
    key = jax.random.fold_in(key, 23)
    key_rows, key_cols = jax.random.split(key, 2)
    entries = jnp.arange(NF_TOT, dtype=jnp.int32)
    device = entries // NF_DEV
    row_ids = device * CL + jax.random.randint(key_rows, (NF_TOT,), 0, CL, dtype=jnp.int32)
    column = jax.random.randint(key_cols, (NF_TOT,), 0, NCL, dtype=jnp.int32)
    return jnp.stack([row_ids, column], 1).astype(jnp.int32)


def shard_levels(own_key, shape, cuts, smallest, top_value):
    def one(axis_at, shards_of):
        steps = jax.random.uniform(jax.random.fold_in(jax.random.fold_in(own_key, 6), axis_at), (shards_of,), jnp.float32, smallest / len(cuts), top_value / len(cuts))
        return jnp.repeat(jnp.exp(steps), shape[axis_at] // shards_of).reshape((-1,) + (1,) * (len(shape) - axis_at - 1))

    level = one(*cuts[0])
    for cut in cuts[1:]:
        level = level * one(*cut)
    return level


def gaussian(own_key, dims, deviation, most, cuts=(), held_as=jnp.bfloat16):
    array = jax.random.normal(own_key, dims, jnp.float32) * deviation
    if len(cuts) > 0:
        array = shard_levels(own_key, dims, cuts, -0.22, 0.18) * array
    return jnp.clip(array, min=-most, max=most).astype(held_as)


def setup_inputs(seed: int = 0, part: int = 0) -> dict:
    seeds = jax.random.split(jax.random.key(seed), 7)
    part_splits = jax.random.split(jax.random.fold_in(seeds[6], part), 7)
    return {
        "right_panel": gaussian(part_splits[0], (NCL, LEAF, COLS), 1.0, 6.0, ((0, 4), (2, 2)), jnp.float32),
        "near_field_blocks": gaussian(part_splits[1], (NB_TOT, LEAF, LEAF), (LEAF * NB_DEV // CL) ** -0.5, 0.1875, ((0, 4), (1, 2))),
        "near_list": draw_near_list(jax.random.fold_in(jax.random.fold_in(seeds[6], part), 71), part),
        "cluster_basis": gaussian(part_splits[3], (NCL, LEAF, RANK), LEAF ** -0.5, 0.375, ((0, 4), (1, 2))),
        "coupling": gaussian(part_splits[4], (NF_TOT, RANK, RANK), (RANK * NF_DEV // CL) ** -0.5, 0.375, ((0, 4),)),
        "far_list": draw_far_list(jax.random.fold_in(jax.random.fold_in(seeds[6], part), 71), part),
    }


def apply_operator(panel_in, near_field_blocks, near_list, cluster_basis, coupling, far_list):
    highest_precision = lax.Precision.HIGHEST
    panel_low = panel_in.astype(jnp.bfloat16)
    basis_wide = cluster_basis.astype(jnp.float32)
    projected = jnp.einsum("nrk,nrc->nkc", basis_wide, panel_low.astype(jnp.float32), precision=highest_precision).astype(jnp.bfloat16)
    far_terms = jnp.einsum("pkr,prc->pkc", coupling.astype(jnp.float32), projected[far_list[:, 1]].astype(jnp.float32), precision=highest_precision)
    far_low = jax.ops.segment_sum(far_terms, far_list[:, 0], num_segments=NCL).astype(jnp.bfloat16)
    result = jnp.einsum("nrk,nkc->nrc", basis_wide, far_low.astype(jnp.float32), precision=highest_precision)

    def add_block(block_index, running):
        start = (block_index * NB_DEV).astype(jnp.int32)
        dense_tile_block = lax.dynamic_slice_in_dim(near_field_blocks, start, NB_DEV, 0)
        pair_block = lax.dynamic_slice_in_dim(near_list, start, NB_DEV, 0)
        source_vector = panel_low[pair_block[:, 1]].astype(jnp.float32)
        term_products = jnp.einsum("fpz,fzg->fpg", dense_tile_block.astype(jnp.float32), source_vector, precision=highest_precision)
        return running + jax.ops.segment_sum(term_products, pair_block[:, 0], num_segments=NCL)

    return lax.fori_loop(0, NB_TOT // NB_DEV, add_block, result)


def reference(right_panel, near_field_blocks, near_list, cluster_basis, coupling, far_list):
    krylov_one = apply_operator(right_panel, near_field_blocks, near_list, cluster_basis, coupling, far_list)
    krylov_two = apply_operator(krylov_one, near_field_blocks, near_list, cluster_basis, coupling, far_list)
    return (krylov_one, krylov_two)
```

```python
import functools

import jax
import jax.numpy as jnp
from jax import lax
from jax.experimental import pallas as pl
from jax.experimental.pallas import tpu as pltpu
from jax.sharding import PartitionSpec as P

UNROLL = 8
VMEM = pl.BlockSpec(memory_space=pltpu.VMEM)
SMEM = pl.BlockSpec(memory_space=pltpu.SMEM)
TRANSPOSED_RHS = (((1,), (1,)), ((), ()))
PLAIN = (((1,), (0,)), ((), ()))


def shifted(array, axis, by):
    size = lax.axis_size(axis)
    return lax.ppermute(array, axis, [(i, (i + by) % size) for i in range(size)])


def dot(a, b, dims):
    return lax.dot_general(a, b, dims, preferred_element_type=jnp.float32)


def params(vmem=48):
    return pltpu.CompilerParams(vmem_limit_bytes=vmem << 20)


def put_projection(low_ref, offset, width, basis_ref, out_ref):
    half = out_ref.shape[0]
    for n in range(half):
        pair = [
            dot(low_ref[m, :, pl.ds(offset, width)], basis_ref[m], TRANSPOSED_RHS)
            for m in (n, n + half)
        ]
        out_ref[n] = jnp.concatenate(pair, 1)


def start_kernel(place_ref, near_ref, panel_ref, basis_ref, low_ref, mine_ref, proj_ref, plan_ref):
    clusters = panel_ref.shape[0]
    slab = basis_ref.shape[2]
    offset = pl.multiple_of(place_ref[1] * slab, slab)
    low_ref[...] = panel_ref[...].astype(jnp.bfloat16)
    mine_ref[...] = low_ref[:, :, pl.ds(offset, slab)]
    put_projection(low_ref, offset, slab, basis_ref, proj_ref)
    for kind in range(3):
        plan_ref[9, kind] = 0

    def sort_entry(t, carry):
        column = near_ref[1, t]
        owner = lax.div(column, clusters)
        kind = lax.rem(owner - place_ref[0] + 1 + place_ref[2], place_ref[2])
        at = plan_ref[9, kind]
        plan_ref[kind, at] = t
        plan_ref[3 + kind, at] = near_ref[0, t] - place_ref[0] * clusters
        plan_ref[6 + kind, at] = column - owner * clusters
        plan_ref[9, kind] = at + 1
        return carry

    lax.fori_loop(0, near_ref.shape[1], sort_entry, 0)
    for kind in range(3):
        count = plan_ref[9, kind]
        for j in range(UNROLL):
            plan_ref[kind, count + j] = 0
            plan_ref[3 + kind, count + j] = clusters
            plan_ref[6 + kind, count + j] = 0


def add_near(plan_ref, kind, source_ref, blocks_ref, offset, width, acc_ref):
    steps = lax.div(plan_ref[9, kind] + UNROLL - 1, UNROLL)

    def step(i, carry):
        terms = []
        for j in range(UNROLL):
            at = i * UNROLL + j
            block = blocks_ref[plan_ref[kind, at], :, pl.ds(offset, width)]
            terms.append(dot(source_ref[plan_ref[6 + kind, at]], block, TRANSPOSED_RHS))
        for j in range(UNROLL):
            row = plan_ref[3 + kind, i * UNROLL + j]
            acc_ref[row] = acc_ref[row] + terms[j]
        return carry

    lax.fori_loop(0, steps, step, 0)


def near_kernel(pieces, first, place_ref, plan_ref, *refs):
    sources, refs = refs[: len(pieces)], refs[len(pieces) :]
    blocks_ref, refs = refs[0], refs[1:]
    acc_ref = refs[-1]
    slab = acc_ref.shape[2]
    if first:
        acc_ref[...] = jnp.zeros_like(acc_ref)
    else:
        acc_ref[...] = refs[0][...]
    for (kind, part), source_ref in zip(pieces, sources):
        width = source_ref.shape[2]
        if part is None:
            offset = 0
        else:
            offset = pl.multiple_of((place_ref[1] if part == 0 else 1 - place_ref[1]) * slab, slab)
        add_near(plan_ref, kind, source_ref, blocks_ref, offset, width, acc_ref)


def far_kernel(place_ref, far_ref, coupling_ref, *refs):
    held, out_ref, unpacked, acc = refs[:-3], refs[-3], refs[-2], refs[-1]
    clusters = out_ref.shape[0]
    half, columns, _ = held[0].shape
    rank = coupling_ref.shape[1]
    for d, packed in enumerate(held):
        unpacked[d * clusters : d * clusters + half] = packed[:, :, :rank]
        unpacked[d * clusters + half : (d + 1) * clusters] = packed[:, :, rank:]
    acc[...] = jnp.zeros_like(acc)

    def step(i, carry):
        terms = []
        for j in range(UNROLL):
            p = i * UNROLL + j
            column = far_ref[1, p]
            owner = lax.div(column, clusters)
            behind = lax.rem(place_ref[0] - owner + place_ref[2], place_ref[2])
            source = unpacked[behind * clusters + column - owner * clusters]
            terms.append(dot(source, coupling_ref[p], TRANSPOSED_RHS))
        for j in range(UNROLL):
            row = far_ref[0, i * UNROLL + j] - place_ref[0] * clusters
            acc[row] = acc[row] + terms[j]
        return carry

    lax.fori_loop(0, coupling_ref.shape[0] // UNROLL, step, 0)
    out_ref[...] = acc[...].astype(jnp.bfloat16)


def finish_kernel(pieces, last, place_ref, plan_ref, *refs):
    count = len(pieces)
    sources, blocks_ref, acc_in, far_ref, basis_ref = refs[:count], *refs[count : count + 4]
    if last:
        out_ref, acc_ref = refs[count + 4 :]
    else:
        out_ref, mine_ref, proj_ref, acc_ref = refs[count + 4 :]
    near_kernel(pieces, False, place_ref, plan_ref, *sources, blocks_ref, acc_in, acc_ref)
    clusters = out_ref.shape[0]
    for n in range(clusters):
        out_ref[n] = acc_ref[n] + dot(far_ref[n], basis_ref[n], PLAIN)
    if not last:
        mine_ref[...] = out_ref[...].astype(jnp.bfloat16)
        put_projection(mine_ref, 0, mine_ref.shape[2], basis_ref, proj_ref)


def tiled_on_device(right_panel, near_field_blocks, near_list, cluster_basis, coupling, far_list):
    clusters, points, columns = right_panel.shape
    near_count = near_list.shape[0]
    slab, rank = cluster_basis.shape[1:]
    panel = right_panel.transpose(0, 2, 1)
    basis = cluster_basis.transpose(0, 2, 1)
    near_list, far_list = near_list.T, far_list.T
    cycle = lax.axis_size("blk")
    place = jnp.stack([lax.axis_index("blk"), lax.axis_index("basis"), jnp.int32(cycle)]).astype(jnp.int32)
    f32, bf16 = jnp.float32, jnp.bfloat16
    mine_shape = jax.ShapeDtypeStruct((clusters, columns, slab), bf16)
    proj_shape = jax.ShapeDtypeStruct((clusters // 2, columns, 2 * rank), f32)
    out_shape = jax.ShapeDtypeStruct((clusters, columns, slab), f32)
    acc_shape = jax.ShapeDtypeStruct((clusters + 1, columns, slab), f32)
    plan_shape = jax.ShapeDtypeStruct((10, near_count + UNROLL), jnp.int32)

    low, mine, proj, plan = pl.pallas_call(
        start_kernel,
        out_shape=(jax.ShapeDtypeStruct((clusters, columns, points), bf16), mine_shape, proj_shape, plan_shape),
        in_specs=[SMEM, SMEM, VMEM, VMEM],
        out_specs=(VMEM, VMEM, VMEM, SMEM),
        compiler_params=params(),
        name="start",
    )(place, near_list, panel, basis)

    def near(pieces, acc, name):
        tags = tuple(tag for tag, _ in pieces)
        operands = [array for _, array in pieces] + [near_field_blocks]
        if acc is not None:
            operands.append(acc)
        return pl.pallas_call(
            functools.partial(near_kernel, tags, acc is None),
            out_shape=acc_shape,
            in_specs=[SMEM, SMEM] + [VMEM] * len(operands),
            out_specs=VMEM,
            compiler_params=params(),
            name=name,
        )(place, plan, *operands)

    def far(held):
        return pl.pallas_call(
            far_kernel,
            out_shape=jax.ShapeDtypeStruct((clusters, columns, rank), bf16),
            in_specs=[SMEM, SMEM, VMEM] + [VMEM] * len(held),
            out_specs=VMEM,
            scratch_shapes=[
                pltpu.VMEM((cycle * clusters, columns, rank), bf16),
                pltpu.VMEM((clusters, columns, rank), f32),
            ],
            compiler_params=params(),
            name="far",
        )(place, far_list, coupling, *held)

    def finish(pieces, acc, far_low, last):
        tags = tuple(tag for tag, _ in pieces)
        outs = (out_shape,) if last else (out_shape, mine_shape, proj_shape)
        operands = [array for _, array in pieces] + [near_field_blocks, acc, far_low, basis]
        return pl.pallas_call(
            functools.partial(finish_kernel, tags, last),
            out_shape=outs,
            in_specs=[SMEM, SMEM] + [VMEM] * len(operands),
            out_specs=(VMEM,) * len(outs),
            scratch_shapes=[pltpu.VMEM(acc_shape.shape, f32)],
            compiler_params=params(),
            name="finish",
        )(place, plan, *operands)

    def projections(proj):
        other = shifted(proj.astype(bf16), "basis", 1)
        whole = (proj + other.astype(f32)).astype(bf16)
        return [whole] + [shifted(whole, "blk", d) for d in range(1, cycle)]

    def apply_operator(mine, proj, own_pieces, last):
        behind, ahead = shifted(mine, "blk", 1), shifted(mine, "blk", -1)
        if own_pieces is None:
            own_pieces = [((1, 0), mine), ((1, 1), shifted(mine, "basis", 1))]
        held = projections(proj)
        acc = near(own_pieces, None, "near_own")
        acc = near([((0, 0), behind), ((2, 0), ahead)], acc, "near_loop")
        far_low = far(held)
        others = [((0, 1), shifted(behind, "basis", 1)), ((2, 1), shifted(ahead, "basis", 1))]
        return finish(others, acc, far_low, last)

    first, mine, proj = apply_operator(mine, proj, [((1, None), low)], False)
    (second,) = apply_operator(mine, proj, None, True)
    return first.transpose(0, 2, 1), second.transpose(0, 2, 1)


def from_behind(array, axis, by):
    size = lax.axis_size(axis)
    return lax.ppermute(array, axis, [(i, (i + by) % size) for i in range(size)])


def general_on_device(right_panel, near_field_blocks, near_list, cluster_basis, coupling, far_list):
    highest_precision = lax.Precision.HIGHEST
    clusters = right_panel.shape[0]
    slab_rows = cluster_basis.shape[1]
    cycle_place = lax.axis_index("blk")
    cycle_size = lax.axis_size("blk")
    basis_owner = lax.axis_index("basis")
    cluster_ids = jnp.arange(clusters, dtype=jnp.int32)
    near_rows = near_list[:, 0] - cycle_place * clusters
    near_cols = near_list[:, 1]
    row_lookup_table = (near_rows[None, :] == cluster_ids[:, None]).astype(jnp.float32)
    far_table = ((far_list[:, 0] - cycle_place * clusters)[None, :] == cluster_ids[:, None]).astype(
        jnp.float32
    )
    slot_index = (
        near_cols // clusters - cycle_place + 1 + cycle_size
    ) % cycle_size * clusters + near_cols % clusters

    def apply_operator(panel_low):
        own_rows = lax.dynamic_slice_in_dim(panel_low, basis_owner * slab_rows, slab_rows, 1)
        partial_sum = jnp.einsum(
            "nrk,nrc->nkc", cluster_basis, own_rows, preferred_element_type=jnp.float32
        )
        projected = lax.psum(partial_sum, "basis").astype(jnp.bfloat16)
        projections_all = lax.all_gather(projected, "blk", axis=0, tiled=True)
        far_terms = jnp.einsum(
            "pkr,prc->pkc",
            coupling,
            projections_all[far_list[:, 1]],
            preferred_element_type=jnp.float32,
        )
        far_sum = jnp.einsum("np,pkc->nkc", far_table, far_terms, precision=highest_precision)
        far_low = far_sum.astype(jnp.bfloat16)
        pieces = []
        for offset in (1, -1):
            pieces.append(from_behind(panel_low, "blk", offset))
        window = jnp.concatenate([pieces[0], panel_low, pieces[1]], 0)
        source_vector = window[slot_index]
        near_field_products = jnp.einsum(
            "fpz,fzg->fpg", near_field_blocks, source_vector, preferred_element_type=jnp.float32
        )
        near_field_total = jnp.einsum(
            "id,dpb->ipb", row_lookup_table, near_field_products, precision=highest_precision
        )
        far_part = jnp.einsum(
            "nrk,nkc->nrc", cluster_basis, far_low, preferred_element_type=jnp.float32
        )
        return far_part + near_field_total

    krylov_one = apply_operator(right_panel.astype(jnp.bfloat16))
    second_low = lax.all_gather(krylov_one.astype(jnp.bfloat16), "basis", axis=1, tiled=True)
    krylov_two = apply_operator(second_low)
    return (krylov_one, krylov_two)


def on_device(right_panel, near_field_blocks, near_list, cluster_basis, coupling, far_list):
    tiled = lax.axis_size("basis") == 2 and cluster_basis.shape[1] % 128 == 0
    run = tiled_on_device if tiled else general_on_device
    return run(right_panel, near_field_blocks, near_list, cluster_basis, coupling, far_list)


def solution(mesh):
    placed = (
        P(("groups", "blk"), None, "col"),
        P(("groups", "blk"), "basis", None),
        P(("groups", "blk"), None),
        P(("groups", "blk"), "basis", None),
        P(("groups", "blk"), None, None),
        P(("groups", "blk"), None),
    )
    return jax.shard_map(
        on_device,
        mesh=mesh,
        in_specs=placed,
        out_specs=(P(("groups", "blk"), "basis", "col"), P(("groups", "blk"), "basis", "col")),
        check_vma=False,
    )
```

```python
import functools

import jax
import jax.numpy as jnp
from jax import lax
from jax.experimental import pallas as pl
from jax.experimental.pallas import tpu as pltpu
from jax.sharding import PartitionSpec as P

UNROLL = 16
FIELD = 9
FAR_UNROLL = 32
VMEM = pl.BlockSpec(memory_space=pltpu.VMEM)
ANY = pl.BlockSpec(memory_space=pl.ANY)
HBM = pl.BlockSpec(memory_space=pltpu.HBM)
SMEM = pl.BlockSpec(memory_space=pltpu.SMEM)
TRANSPOSED_RHS = (((1,), (1,)), ((), ()))
PLAIN = (((1,), (0,)), ((), ()))


def swapped(array, axis, partner):
    return lax.ppermute(array, axis, [(i, partner(i)) for i in range(lax.axis_size(axis))])


def dot(a, b, dims):
    return lax.dot_general(a, b, dims, preferred_element_type=jnp.float32)


def params(mebibytes=14):
    return pltpu.CompilerParams(vmem_limit_bytes=mebibytes << 20)


def in_hbm(array):
    return pltpu.with_memory_space_constraint(array, pltpu.HBM)


def cost(microseconds):
    return pl.CostEstimate(flops=0, transcendentals=0, bytes_accessed=int(microseconds * 3.69e6))


def put_projection(place_ref, low_ref, basis_ref, keep_ref, send_ref, at, parts):
    quarter = keep_ref.shape[0]
    for part in range(2):
        for n in range(quarter):
            m = 2 * part * quarter + n
            pair = [dot(low_ref[i], basis_ref[i], TRANSPOSED_RHS) for i in (m, m + quarter)]
            parts[part, n] = jnp.concatenate(pair, 1)
    keep_ref[...] = parts[place_ref[1]]
    send_ref[at:] = parts[1 - place_ref[1]].astype(jnp.bfloat16)


def start_kernel(place_ref, panel_hbm, basis_hbm, mine_ref, basis_ref, keep_ref, send_ref, panel, parts, arrived):
    slab = basis_ref.shape[2]
    offset = pl.multiple_of(place_ref[1] * slab, slab)
    pieces = arrived.shape[0] // 2
    size = panel.shape[0] // pieces
    for i in range(pieces):
        rows = pl.ds(i * size, size)
        pltpu.make_async_copy(panel_hbm.at[rows, :, pl.ds(offset, slab)], panel.at[rows], arrived.at[i]).start()
        pltpu.make_async_copy(basis_hbm.at[rows], basis_ref.at[rows], arrived.at[pieces + i]).start()
    for i in range(pieces):
        rows = pl.ds(i * size, size)
        pltpu.make_async_copy(panel_hbm.at[rows, :, pl.ds(offset, slab)], panel.at[rows], arrived.at[i]).wait()
        mine_ref[rows] = panel[rows].astype(jnp.bfloat16)
    for i in range(pieces):
        rows = pl.ds(i * size, size)
        pltpu.make_async_copy(basis_hbm.at[rows], basis_ref.at[rows], arrived.at[pieces + i]).wait()
    put_projection(place_ref, mine_ref, basis_ref, keep_ref, send_ref, 0, parts)


def put_sorted(words_ref, kinds, nothing, plan_ref):
    count, width = words_ref.shape[1], plan_ref.shape[1]
    across = jnp.broadcast_to(words_ref[...], (count, count))
    down = across.T
    kind_across, kind_down = lax.shift_right_logical(across, 3 * FIELD), lax.shift_right_logical(down, 3 * FIELD)
    t = lax.broadcasted_iota(jnp.int32, (count, count), 1)
    s = lax.broadcasted_iota(jnp.int32, (count, count), 0)
    before = jnp.sum(((kind_across == kind_down) & (t < s)).astype(jnp.float32), 1, keepdims=True).astype(jnp.int32)
    word = down[:, :1]
    place = lax.broadcasted_iota(jnp.int32, (count, width), 1)
    slot = lax.broadcasted_iota(jnp.int32, (1, width), 1)
    totals = jnp.zeros((1, width), jnp.int32)
    for kind in range(kinds):
        of_kind = kind_down[:, :1] == kind
        total = jnp.sum(of_kind.astype(jnp.float32), 0, keepdims=True).astype(jnp.int32)
        row = jnp.sum(jnp.where(of_kind & (before == place), word, 0), 0, keepdims=True)
        plan_ref[kind : kind + 1] = jnp.where(slot < total, row, nothing)
        totals = jnp.where(slot == kind, total, totals)
    plan_ref[kinds : kinds + 1] = totals


def plan_kernel(nothing, near_ref, far_ref, near_plan_ref, far_plan_ref):
    put_sorted(near_ref, 3, nothing, near_plan_ref)
    put_sorted(far_ref, 2, nothing, far_plan_ref)


def prepare_kernel(far_plan_ref, blocks_hbm, coupling_hbm, blocks_ref, pairs_ref, coupling, turned, arrived):
    pieces = arrived.shape[0] - 1
    size = blocks_ref.shape[0] // pieces
    first = pltpu.make_async_copy(coupling_hbm, coupling, arrived.at[pieces])
    first.start()
    copies = [
        pltpu.make_async_copy(
            blocks_hbm.at[pl.ds(i * size, size)], blocks_ref.at[pl.ds(i * size, size)], arrived.at[i]
        )
        for i in range(pieces)
    ]
    for copy in copies:
        copy.start()
    first.wait()
    rank, _, count = coupling.shape
    for k in range(rank):
        turned[k * count : (k + 1) * count] = coupling[k].astype(jnp.float32).T

    def step(i, carry):
        for j in range(FAR_UNROLL):
            at = i * FAR_UNROLL + j
            pair = lax.shift_right_logical(far_plan_ref[0, at], 2 * FIELD) & ((1 << FIELD) - 1)
            pairs_ref[at] = turned[pl.ds(pair, rank, stride=count)].astype(jnp.bfloat16)
        return carry

    lax.fori_loop(0, lax.div(far_plan_ref[2, 0] + FAR_UNROLL - 1, FAR_UNROLL), step, 0)
    for copy in copies:
        copy.wait()


def add_near(plan_ref, kind, source_ref, blocks_ref, acc_ref):
    mask = (1 << FIELD) - 1

    def step(i, carry):
        words = [plan_ref[kind, i * UNROLL + j] for j in range(UNROLL)]
        terms = []
        for word in words:
            block = blocks_ref[lax.shift_right_logical(word, 2 * FIELD) & mask]
            terms.append(dot(source_ref[word & mask], block, TRANSPOSED_RHS))
        for word, term in zip(words, terms):
            row = lax.shift_right_logical(word, FIELD) & mask
            acc_ref[row] = acc_ref[row] + term
        return carry

    lax.fori_loop(0, lax.div(plan_ref[3, kind] + UNROLL - 1, UNROLL), step, 0)


def near_own_kernel(plan_ref, panel_hbm, blocks_ref, acc_ref, panel, low, arrived):
    copy = pltpu.make_async_copy(panel_hbm, panel, arrived)
    copy.start()
    acc_ref[...] = jnp.zeros_like(acc_ref)
    copy.wait()
    low[...] = panel[...].astype(jnp.bfloat16)
    add_near(plan_ref, 0, low, blocks_ref, acc_ref)


def put_whole(place_ref, same_ref, other_ref, whole):
    slab = same_ref.shape[2]
    first = place_ref[1] == 0
    same, other = same_ref[...], other_ref[: same_ref.shape[0]]
    whole[:, :, :slab] = jnp.where(first, same, other)
    whole[:, :, slab:] = jnp.where(first, other, same)


def near_halves_kernel(kind, place_ref, plan_ref, same_ref, other_ref, blocks_ref, *refs):
    acc_ref, whole = refs[-2:]
    put_whole(place_ref, same_ref, other_ref, whole)
    acc_ref[...] = refs[0][...] if len(refs) == 3 else jnp.zeros_like(acc_ref)
    add_near(plan_ref, kind, whole, blocks_ref, acc_ref)


def far_kernel(plan_ref, pairs_ref, *refs):
    held, keep_ref, send_ref, unpacked, acc = refs[:-4], *refs[-4:]
    clusters = keep_ref.shape[0]
    quarter = held[0].shape[0]
    rank = pairs_ref.shape[1]
    mask = (1 << FIELD) - 1
    for d, packed in enumerate(held):
        unpacked[2 * d * quarter : (2 * d + 1) * quarter] = packed[:, :, :rank]
        unpacked[(2 * d + 1) * quarter : (2 * d + 2) * quarter] = packed[:, :, rank:]
    acc[...] = jnp.zeros_like(acc)

    def step(i, carry):
        words = [plan_ref[0, i * FAR_UNROLL + j] for j in range(FAR_UNROLL)]
        terms = []
        for j, word in enumerate(words):
            terms.append(dot(unpacked[word & mask], pairs_ref[i * FAR_UNROLL + j], TRANSPOSED_RHS))
        for word, term in zip(words, terms):
            row = lax.shift_right_logical(word, FIELD) & mask
            acc[row] = acc[row] + term
        return carry

    lax.fori_loop(0, lax.div(plan_ref[2, 0] + FAR_UNROLL - 1, FAR_UNROLL), step, 0)
    half = clusters // 2
    for n in range(half):
        keep_ref[n] = acc[n]
        keep_ref[n + half] = acc[n + half]
        send_ref[n] = jnp.concatenate([acc[n], acc[n + half]], 1).astype(jnp.bfloat16)


def finish_kernel(place_ref, plan_ref, same_ref, other_ref, blocks_ref, acc_in, far_ref, far_other_ref, basis_ref, *refs):
    out_ref, (acc_ref, whole) = refs[0], refs[-2:]
    near_halves_kernel(2, place_ref, plan_ref, same_ref, other_ref, blocks_ref, acc_in, acc_ref, whole)
    half, _, wide = far_other_ref.shape
    rank = wide // 2
    for n in range(half):
        for m, other in ((n, far_other_ref[n, :, :rank]), (n + half, far_other_ref[n, :, rank:])):
            far_low = (far_ref[m] + other.astype(jnp.float32)).astype(jnp.bfloat16)
            out_ref[m] = acc_ref[m] + dot(far_low, basis_ref[m], PLAIN)
    if len(refs) == 7:
        mine_ref, keep_ref, send_ref, parts = refs[1:5]
        low = out_ref[...].astype(jnp.bfloat16)
        mine_ref[...] = low
        send_ref[: 2 * half] = low
        put_projection(place_ref, mine_ref, basis_ref, keep_ref, send_ref, 2 * half, parts)


def tiled_on_device(right_panel, near_field_blocks, near_list, cluster_basis, coupling, far_list):
    clusters, points, columns = right_panel.shape
    near_count = near_list.shape[0]
    slab, rank = cluster_basis.shape[1:]
    panel = right_panel.transpose(0, 2, 1)
    basis = cluster_basis.transpose(0, 2, 1)
    cycle = lax.axis_size("blk")
    place = jnp.stack([lax.axis_index("blk"), lax.axis_index("basis")]).astype(jnp.int32)
    half, quarter = clusters // 2, clusters // 4
    near_owner, far_owner = near_list[:, 1] // clusters, far_list[:, 1] // clusters
    words = jnp.where(near_owner == place[0], 0, jnp.where(near_owner == place[0] ^ 1, 1, 2))
    words = words << FIELD | jnp.arange(near_count, dtype=jnp.int32)
    words = words << FIELD | near_list[:, 0] - place[0] * clusters
    words = words << FIELD | near_list[:, 1] % clusters
    far_source = far_list[:, 1] % clusters
    far_words = (far_source // half != place[1]).astype(jnp.int32)
    far_words = far_words << FIELD | jnp.arange(far_list.shape[0], dtype=jnp.int32)
    far_words = far_words << FIELD | far_list[:, 0] - place[0] * clusters
    far_words = far_words << FIELD | (place[0] ^ far_owner) * half + far_source % half
    f32, bf16 = jnp.float32, jnp.bfloat16
    mine_shape = jax.ShapeDtypeStruct((clusters, columns, slab), bf16)
    keep_shape = jax.ShapeDtypeStruct((quarter, columns, 2 * rank), f32)
    send_shape = jax.ShapeDtypeStruct((quarter, columns, 2 * rank), bf16)
    both_shape = jax.ShapeDtypeStruct((clusters + quarter, columns, slab), bf16)
    parts = pltpu.VMEM((2, quarter, columns, 2 * rank), f32)
    out_shape = jax.ShapeDtypeStruct((clusters, columns, slab), f32)
    acc_shape = jax.ShapeDtypeStruct((clusters + 1, columns, slab), f32)
    near_plan_shape = jax.ShapeDtypeStruct((4, near_count + UNROLL), jnp.int32)
    far_plan_shape = jax.ShapeDtypeStruct((3, far_list.shape[0] + FAR_UNROLL), jnp.int32)

    low_shape = jax.ShapeDtypeStruct((clusters, columns, points), bf16)
    pieces = 4
    mine, basis, keep, send = pl.pallas_call(
        start_kernel,
        out_shape=(mine_shape, jax.ShapeDtypeStruct(basis.shape, bf16), keep_shape, send_shape),
        in_specs=[SMEM, HBM, HBM],
        out_specs=(VMEM,) * 4,
        scratch_shapes=[pltpu.VMEM(mine_shape.shape, f32), parts, pltpu.SemaphoreType.DMA((2 * pieces,))],
        compiler_params=params(),
        cost_estimate=cost(2),
        name="start",
    )(place, in_hbm(panel), in_hbm(basis))
    near_plan, far_plan = pl.pallas_call(
        functools.partial(plan_kernel, clusters << FIELD),
        out_shape=(near_plan_shape, far_plan_shape),
        in_specs=[VMEM, VMEM],
        out_specs=(VMEM, VMEM),
        compiler_params=params(),
        cost_estimate=cost(1),
        name="plan",
    )(words[None], far_words[None])
    blocks, pairs = pl.pallas_call(
        prepare_kernel,
        out_shape=(
            pltpu.VMEM(near_field_blocks.shape, bf16),
            pltpu.VMEM((coupling.shape[0] + FAR_UNROLL, rank, rank), bf16),
        ),
        in_specs=[SMEM, HBM, HBM],
        out_specs=(VMEM, VMEM),
        scratch_shapes=[
            pltpu.VMEM((rank, rank, coupling.shape[0]), bf16),
            pltpu.VMEM((rank * coupling.shape[0], rank), f32),
            pltpu.SemaphoreType.DMA((9,)),
        ],
        compiler_params=params(20),
        cost_estimate=cost(4),
        name="prepare",
    )(far_plan, in_hbm(near_field_blocks), in_hbm(coupling.transpose(1, 2, 0)))

    def near_own(plan, blocks):
        return pl.pallas_call(
            near_own_kernel,
            out_shape=acc_shape,
            in_specs=[SMEM, HBM, VMEM],
            out_specs=VMEM,
            scratch_shapes=[
                pltpu.VMEM(panel.shape, f32),
                pltpu.VMEM(low_shape.shape, bf16),
                pltpu.SemaphoreType.DMA,
            ],
            compiler_params=params(),
            cost_estimate=cost(3),
            name="near_own",
        )(plan, panel, blocks)

    def near_halves(plan, blocks, kind, same, other, *acc):
        return pl.pallas_call(
            functools.partial(near_halves_kernel, kind),
            out_shape=acc_shape,
            in_specs=[SMEM, SMEM] + [VMEM] * (3 + len(acc)),
            out_specs=VMEM,
            scratch_shapes=[pltpu.VMEM(low_shape.shape, bf16)],
            compiler_params=params(),
            cost_estimate=cost(2),
            name="near_halves",
        )(place, plan, same, other, blocks, *acc)

    def far(plan, held):
        return pl.pallas_call(
            far_kernel,
            out_shape=(
                jax.ShapeDtypeStruct((clusters, columns, rank), f32),
                jax.ShapeDtypeStruct((half, columns, 2 * rank), bf16),
            ),
            in_specs=[SMEM, VMEM] + [VMEM] * len(held),
            out_specs=(VMEM, VMEM),
            scratch_shapes=[
                pltpu.VMEM((cycle * half, columns, rank), bf16),
                pltpu.VMEM((clusters + 1, columns, rank), f32),
            ],
            compiler_params=params(),
            cost_estimate=cost(3),
            name="far",
        )(plan, pairs, *held)

    def finish(plan, blocks, same, other, acc, far_sum, far_other, last):
        outs = (out_shape,) if last else (out_shape, mine_shape, keep_shape, both_shape)
        return pl.pallas_call(
            finish_kernel,
            out_shape=outs,
            in_specs=[SMEM, SMEM] + [VMEM] * 7,
            out_specs=(VMEM,) * len(outs),
            scratch_shapes=([] if last else [parts])
            + [pltpu.VMEM(acc_shape.shape, f32), pltpu.VMEM(low_shape.shape, bf16)],
            compiler_params=params(),
            cost_estimate=cost(4),
            name="finish",
        )(place, plan, same, other, blocks, acc, far_sum, far_other, basis)

    def other_basis(array):
        return swapped(array, "basis", lambda i: 1 - i)

    def apply_operator(mine, keep, send, near_plan, last):
        between = swapped(mine, "blk", lambda i: (((i + 1) % cycle ^ 1) - 1) % cycle)
        paired = swapped(mine, "blk", lambda i: i ^ 1)
        received = other_basis(send)
        if last:
            acc = near_halves(near_plan, blocks, 0, mine, received)
        else:
            acc = near_own(near_plan, blocks)
        held = [(keep + received[-quarter:].astype(f32)).astype(bf16)]
        held += [swapped(held[0], "blk", lambda i, d=d: i ^ d) for d in range(1, cycle)]
        paired, acc = lax.optimization_barrier((paired, acc))
        between, *held = lax.optimization_barrier((between, *held))
        paired_other = other_basis(paired)
        between_other = other_basis(between)
        far_sum, far_send = far(far_plan, held)
        far_other = other_basis(far_send)
        acc = near_halves(near_plan, blocks, 1, paired, paired_other, acc)
        return finish(near_plan, blocks, between, between_other, acc, far_sum, far_other, last), near_plan

    (first, mine, keep, send), near_plan = apply_operator(mine, keep, send, near_plan, False)
    (second,), _ = apply_operator(mine, keep, send, near_plan, True)
    return first.transpose(0, 2, 1), second.transpose(0, 2, 1)


def from_behind(array, axis, by):
    size = lax.axis_size(axis)
    return lax.ppermute(array, axis, [(i, (i + by) % size) for i in range(size)])


def general_on_device(right_panel, near_field_blocks, near_list, cluster_basis, coupling, far_list):
    highest_precision = lax.Precision.HIGHEST
    clusters = right_panel.shape[0]
    slab_rows = cluster_basis.shape[1]
    cycle_place = lax.axis_index("blk")
    cycle_size = lax.axis_size("blk")
    basis_owner = lax.axis_index("basis")
    cluster_ids = jnp.arange(clusters, dtype=jnp.int32)
    near_rows = near_list[:, 0] - cycle_place * clusters
    near_cols = near_list[:, 1]
    row_lookup_table = (near_rows[None, :] == cluster_ids[:, None]).astype(jnp.float32)
    far_table = ((far_list[:, 0] - cycle_place * clusters)[None, :] == cluster_ids[:, None]).astype(
        jnp.float32
    )
    slot_index = (
        near_cols // clusters - cycle_place + 1 + cycle_size
    ) % cycle_size * clusters + near_cols % clusters

    def apply_operator(panel_low):
        own_rows = lax.dynamic_slice_in_dim(panel_low, basis_owner * slab_rows, slab_rows, 1)
        partial_sum = jnp.einsum(
            "nrk,nrc->nkc", cluster_basis, own_rows, preferred_element_type=jnp.float32
        )
        projected = lax.psum(partial_sum, "basis").astype(jnp.bfloat16)
        projections_all = lax.all_gather(projected, "blk", axis=0, tiled=True)
        far_terms = jnp.einsum(
            "pkr,prc->pkc",
            coupling,
            projections_all[far_list[:, 1]],
            preferred_element_type=jnp.float32,
        )
        far_sum = jnp.einsum("np,pkc->nkc", far_table, far_terms, precision=highest_precision)
        far_low = far_sum.astype(jnp.bfloat16)
        pieces = []
        for offset in (1, -1):
            pieces.append(from_behind(panel_low, "blk", offset))
        window = jnp.concatenate([pieces[0], panel_low, pieces[1]], 0)
        source_vector = window[slot_index]
        near_field_products = jnp.einsum(
            "fpz,fzg->fpg", near_field_blocks, source_vector, preferred_element_type=jnp.float32
        )
        near_field_total = jnp.einsum(
            "id,dpb->ipb", row_lookup_table, near_field_products, precision=highest_precision
        )
        far_part = jnp.einsum(
            "nrk,nkc->nrc", cluster_basis, far_low, preferred_element_type=jnp.float32
        )
        return far_part + near_field_total

    krylov_one = apply_operator(right_panel.astype(jnp.bfloat16))
    second_low = lax.all_gather(krylov_one.astype(jnp.bfloat16), "basis", axis=1, tiled=True)
    krylov_two = apply_operator(second_low)
    return (krylov_one, krylov_two)


def on_device(right_panel, near_field_blocks, near_list, cluster_basis, coupling, far_list):
    cycle = lax.axis_size("blk")
    tiled = lax.axis_size("basis") == 2 and cluster_basis.shape[1] % 128 == 0 and cycle & (cycle - 1) == 0
    run = tiled_on_device if tiled else general_on_device
    return run(right_panel, near_field_blocks, near_list, cluster_basis, coupling, far_list)


def solution(mesh):
    placed = (
        P(("groups", "blk"), None, "col"),
        P(("groups", "blk"), "basis", None),
        P(("groups", "blk"), None),
        P(("groups", "blk"), "basis", None),
        P(("groups", "blk"), None, None),
        P(("groups", "blk"), None),
    )
    return jax.shard_map(
        on_device,
        mesh=mesh,
        in_specs=placed,
        out_specs=(P(("groups", "blk"), "basis", "col"), P(("groups", "blk"), "basis", "col")),
        check_vma=False,
    )
```

```python
import functools

import jax
import jax.numpy as jnp
from jax import lax
from jax.experimental import pallas as pl
from jax.experimental.pallas import tpu as pltpu
from jax.sharding import PartitionSpec as P

UNROLL = 16
FIELD = 9
FAR_UNROLL = 32
VMEM = pl.BlockSpec(memory_space=pltpu.VMEM)
ANY = pl.BlockSpec(memory_space=pl.ANY)
HBM = pl.BlockSpec(memory_space=pltpu.HBM)
SMEM = pl.BlockSpec(memory_space=pltpu.SMEM)
TRANSPOSED_RHS = (((1,), (1,)), ((), ()))
PLAIN = (((1,), (0,)), ((), ()))


def swapped(array, axis, partner):
    return lax.ppermute(array, axis, [(i, partner(i)) for i in range(lax.axis_size(axis))])


def dot(a, b, dims):
    return lax.dot_general(a, b, dims, preferred_element_type=jnp.float32)


def params(mebibytes=14):
    return pltpu.CompilerParams(vmem_limit_bytes=mebibytes << 20)


def in_smem(array):
    return pltpu.with_memory_space_constraint(array, pltpu.SMEM)


def in_hbm(array):
    return pltpu.with_memory_space_constraint(array, pltpu.HBM)


def cost(microseconds):
    return pl.CostEstimate(flops=0, transcendentals=0, bytes_accessed=int(microseconds * 3.69e6))


def put_projection(low_ref, basis_ref, keep_ref, send_ref, at, parts):
    quarter = keep_ref.shape[0]
    for part in range(2):
        for n in range(quarter):
            m = 2 * part * quarter + n
            pair = [dot(low_ref[i], basis_ref[i], TRANSPOSED_RHS) for i in (m, m + quarter)]
            parts[part, n] = jnp.concatenate(pair, 1)
    keep_ref[...] = parts[lax.axis_index("basis")]
    send_ref[at:] = parts[1 - lax.axis_index("basis")].astype(jnp.bfloat16)


def start_kernel(panel_hbm, basis_hbm, mine_ref, basis_ref, keep_ref, send_ref, panel, parts, arrived):
    slab = basis_ref.shape[2]
    offset = pl.multiple_of(lax.axis_index("basis") * slab, slab)
    pieces = arrived.shape[0] // 2
    size = panel.shape[0] // pieces
    for i in range(pieces):
        rows = pl.ds(i * size, size)
        pltpu.make_async_copy(panel_hbm.at[rows, :, pl.ds(offset, slab)], panel.at[rows], arrived.at[i]).start()
        pltpu.make_async_copy(basis_hbm.at[rows], basis_ref.at[rows], arrived.at[pieces + i]).start()
    for i in range(pieces):
        rows = pl.ds(i * size, size)
        pltpu.make_async_copy(panel_hbm.at[rows, :, pl.ds(offset, slab)], panel.at[rows], arrived.at[i]).wait()
        mine_ref[rows] = panel[rows].astype(jnp.bfloat16)
    for i in range(pieces):
        rows = pl.ds(i * size, size)
        pltpu.make_async_copy(basis_hbm.at[rows], basis_ref.at[rows], arrived.at[pieces + i]).wait()
    put_projection(mine_ref, basis_ref, keep_ref, send_ref, 0, parts)


def put_sorted(words_ref, kinds, nothing, plan_ref):
    count, width = words_ref.shape[1], plan_ref.shape[1]
    across = jnp.broadcast_to(words_ref[...], (count, count))
    down = across.T
    kind_across, kind_down = lax.shift_right_logical(across, 3 * FIELD), lax.shift_right_logical(down, 3 * FIELD)
    t = lax.broadcasted_iota(jnp.int32, (count, count), 1)
    s = lax.broadcasted_iota(jnp.int32, (count, count), 0)
    before = jnp.sum(((kind_across == kind_down) & (t < s)).astype(jnp.float32), 1, keepdims=True).astype(jnp.int32)
    word = down[:, :1]
    place = lax.broadcasted_iota(jnp.int32, (count, width), 1)
    slot = lax.broadcasted_iota(jnp.int32, (1, width), 1)
    totals = jnp.zeros((1, width), jnp.int32)
    for kind in range(kinds):
        of_kind = kind_down[:, :1] == kind
        total = jnp.sum(of_kind.astype(jnp.float32), 0, keepdims=True).astype(jnp.int32)
        row = jnp.sum(jnp.where(of_kind & (before == place), word, 0), 0, keepdims=True)
        plan_ref[kind : kind + 1] = jnp.where(slot < total, row, nothing)
        totals = jnp.where(slot == kind, total, totals)
    plan_ref[kinds : kinds + 1] = totals


def plan_kernel(nothing, near_ref, far_ref, near_plan_ref, far_plan_ref, near_plan, far_plan, sent):
    put_sorted(near_ref, 3, nothing, near_plan)
    put_sorted(far_ref, 2, nothing, far_plan)
    near_copy = pltpu.make_async_copy(near_plan, near_plan_ref, sent.at[0])
    far_copy = pltpu.make_async_copy(far_plan, far_plan_ref, sent.at[1])
    near_copy.start()
    far_copy.start()
    near_copy.wait()
    far_copy.wait()


def prepare_kernel(far_plan_ref, blocks_hbm, coupling_hbm, blocks_ref, pairs_ref, coupling, turned, arrived):
    pieces = arrived.shape[0] - 1
    size = blocks_ref.shape[0] // pieces
    first = pltpu.make_async_copy(coupling_hbm, coupling, arrived.at[pieces])
    first.start()
    copies = [
        pltpu.make_async_copy(
            blocks_hbm.at[pl.ds(i * size, size)], blocks_ref.at[pl.ds(i * size, size)], arrived.at[i]
        )
        for i in range(pieces)
    ]
    for copy in copies:
        copy.start()
    first.wait()
    rank, _, count = coupling.shape
    for k in range(rank):
        turned[k * count : (k + 1) * count] = coupling[k].astype(jnp.float32).T

    def step(i, carry):
        for j in range(FAR_UNROLL):
            at = i * FAR_UNROLL + j
            pair = lax.shift_right_logical(far_plan_ref[0, at], 2 * FIELD) & ((1 << FIELD) - 1)
            pairs_ref[at] = turned[pl.ds(pair, rank, stride=count)].astype(jnp.bfloat16)
        return carry

    lax.fori_loop(0, lax.div(far_plan_ref[2, 0] + FAR_UNROLL - 1, FAR_UNROLL), step, 0)
    for copy in copies:
        copy.wait()


def add_near(plan_ref, kind, source_ref, blocks_ref, acc_ref):
    mask = (1 << FIELD) - 1

    def step(i, carry):
        words = [plan_ref[kind, i * UNROLL + j] for j in range(UNROLL)]
        terms = []
        for word in words:
            block = blocks_ref[lax.shift_right_logical(word, 2 * FIELD) & mask]
            terms.append(dot(source_ref[word & mask], block, TRANSPOSED_RHS))
        for word, term in zip(words, terms):
            row = lax.shift_right_logical(word, FIELD) & mask
            acc_ref[row] = acc_ref[row] + term
        return carry

    lax.fori_loop(0, lax.div(plan_ref[3, kind] + UNROLL - 1, UNROLL), step, 0)


def near_own_kernel(plan_ref, panel_hbm, blocks_ref, acc_ref, panel, low, arrived):
    copy = pltpu.make_async_copy(panel_hbm, panel, arrived)
    copy.start()
    acc_ref[...] = jnp.zeros_like(acc_ref)
    copy.wait()
    low[...] = panel[...].astype(jnp.bfloat16)
    add_near(plan_ref, 0, low, blocks_ref, acc_ref)


def put_whole(same_ref, other_ref, whole):
    slab = same_ref.shape[2]
    first = lax.axis_index("basis") == 0
    same, other = same_ref[...], other_ref[: same_ref.shape[0]]
    whole[:, :, :slab] = jnp.where(first, same, other)
    whole[:, :, slab:] = jnp.where(first, other, same)


def near_halves_kernel(kind, plan_ref, same_ref, other_ref, blocks_ref, *refs):
    acc_ref, whole = refs[-2:]
    put_whole(same_ref, other_ref, whole)
    acc_ref[...] = refs[0][...] if len(refs) == 3 else jnp.zeros_like(acc_ref)
    add_near(plan_ref, kind, whole, blocks_ref, acc_ref)


def far_kernel(plan_ref, pairs_ref, *refs):
    held, keep_ref, send_ref, unpacked, acc = refs[:-4], *refs[-4:]
    clusters = keep_ref.shape[0]
    quarter = held[0].shape[0]
    rank = pairs_ref.shape[1]
    mask = (1 << FIELD) - 1
    for d, packed in enumerate(held):
        unpacked[2 * d * quarter : (2 * d + 1) * quarter] = packed[:, :, :rank]
        unpacked[(2 * d + 1) * quarter : (2 * d + 2) * quarter] = packed[:, :, rank:]
    acc[...] = jnp.zeros_like(acc)

    def step(i, carry):
        words = [plan_ref[0, i * FAR_UNROLL + j] for j in range(FAR_UNROLL)]
        terms = []
        for j, word in enumerate(words):
            terms.append(dot(unpacked[word & mask], pairs_ref[i * FAR_UNROLL + j], TRANSPOSED_RHS))
        for word, term in zip(words, terms):
            row = lax.shift_right_logical(word, FIELD) & mask
            acc[row] = acc[row] + term
        return carry

    lax.fori_loop(0, lax.div(plan_ref[2, 0] + FAR_UNROLL - 1, FAR_UNROLL), step, 0)
    half = clusters // 2
    for n in range(half):
        keep_ref[n] = acc[n]
        keep_ref[n + half] = acc[n + half]
        send_ref[n] = jnp.concatenate([acc[n], acc[n + half]], 1).astype(jnp.bfloat16)


def finish_kernel(plan_ref, same_ref, other_ref, blocks_ref, acc_in, far_ref, far_other_ref, basis_ref, *refs):
    out_ref, (acc_ref, whole) = refs[0], refs[-2:]
    near_halves_kernel(2, plan_ref, same_ref, other_ref, blocks_ref, acc_in, acc_ref, whole)
    half, _, wide = far_other_ref.shape
    rank = wide // 2
    for n in range(half):
        for m, other in ((n, far_other_ref[n, :, :rank]), (n + half, far_other_ref[n, :, rank:])):
            far_low = (far_ref[m] + other.astype(jnp.float32)).astype(jnp.bfloat16)
            out_ref[m] = acc_ref[m] + dot(far_low, basis_ref[m], PLAIN)
    if len(refs) == 7:
        mine_ref, keep_ref, send_ref, parts = refs[1:5]
        low = out_ref[...].astype(jnp.bfloat16)
        mine_ref[...] = low
        send_ref[: 2 * half] = low
        put_projection(mine_ref, basis_ref, keep_ref, send_ref, 2 * half, parts)


def tiled_on_device(right_panel, near_field_blocks, near_list, cluster_basis, coupling, far_list):
    clusters, points, columns = right_panel.shape
    near_count = near_list.shape[0]
    slab, rank = cluster_basis.shape[1:]
    panel = right_panel.transpose(0, 2, 1)
    basis = cluster_basis.transpose(0, 2, 1)
    cycle = lax.axis_size("blk")
    place = jnp.stack([lax.axis_index("blk"), lax.axis_index("basis")]).astype(jnp.int32)
    half, quarter = clusters // 2, clusters // 4
    near_owner, far_owner = near_list[:, 1] // clusters, far_list[:, 1] // clusters
    words = jnp.where(near_owner == place[0], 0, jnp.where(near_owner == place[0] ^ 1, 2, 1))
    words = words << FIELD | jnp.arange(near_count, dtype=jnp.int32)
    words = words << FIELD | near_list[:, 0] - place[0] * clusters
    words = words << FIELD | near_list[:, 1] % clusters
    far_source = far_list[:, 1] % clusters
    far_words = (far_source // half != place[1]).astype(jnp.int32)
    far_words = far_words << FIELD | jnp.arange(far_list.shape[0], dtype=jnp.int32)
    far_words = far_words << FIELD | far_list[:, 0] - place[0] * clusters
    far_words = far_words << FIELD | (place[0] ^ far_owner) * half + far_source % half
    f32, bf16 = jnp.float32, jnp.bfloat16
    mine_shape = jax.ShapeDtypeStruct((clusters, columns, slab), bf16)
    keep_shape = jax.ShapeDtypeStruct((quarter, columns, 2 * rank), f32)
    send_shape = jax.ShapeDtypeStruct((quarter, columns, 2 * rank), bf16)
    both_shape = jax.ShapeDtypeStruct((clusters + quarter, columns, slab), bf16)
    parts = pltpu.VMEM((2, quarter, columns, 2 * rank), f32)
    out_shape = jax.ShapeDtypeStruct((clusters, columns, slab), f32)
    acc_shape = jax.ShapeDtypeStruct((clusters + 1, columns, slab), f32)
    near_plan_shape = jax.ShapeDtypeStruct((4, near_count + UNROLL), jnp.int32)
    far_plan_shape = jax.ShapeDtypeStruct((3, far_list.shape[0] + FAR_UNROLL), jnp.int32)

    low_shape = jax.ShapeDtypeStruct((clusters, columns, points), bf16)
    pieces = 4
    mine, basis, keep, send = pl.pallas_call(
        start_kernel,
        out_shape=(mine_shape, jax.ShapeDtypeStruct(basis.shape, bf16), keep_shape, send_shape),
        in_specs=[HBM, HBM],
        out_specs=(VMEM,) * 4,
        scratch_shapes=[pltpu.VMEM(mine_shape.shape, f32), parts, pltpu.SemaphoreType.DMA((2 * pieces,))],
        compiler_params=params(),
        cost_estimate=cost(2),
        name="start",
    )(in_hbm(panel), in_hbm(basis))
    near_plan, far_plan = pl.pallas_call(
        functools.partial(plan_kernel, clusters << FIELD),
        out_shape=(
            pltpu.SMEM(near_plan_shape.shape, jnp.int32),
            pltpu.SMEM(far_plan_shape.shape, jnp.int32),
        ),
        in_specs=[VMEM, VMEM],
        out_specs=(SMEM, SMEM),
        scratch_shapes=[
            pltpu.VMEM(near_plan_shape.shape, jnp.int32),
            pltpu.VMEM(far_plan_shape.shape, jnp.int32),
            pltpu.SemaphoreType.DMA((2,)),
        ],
        compiler_params=params(),
        cost_estimate=cost(1),
        name="plan",
    )(words[None], far_words[None])
    blocks, pairs = pl.pallas_call(
        prepare_kernel,
        out_shape=(
            pltpu.VMEM(near_field_blocks.shape, bf16),
            pltpu.VMEM((coupling.shape[0] + FAR_UNROLL, rank, rank), bf16),
        ),
        in_specs=[SMEM, HBM, HBM],
        out_specs=(VMEM, VMEM),
        scratch_shapes=[
            pltpu.VMEM((rank, rank, coupling.shape[0]), bf16),
            pltpu.VMEM((rank * coupling.shape[0], rank), f32),
            pltpu.SemaphoreType.DMA((9,)),
        ],
        compiler_params=params(20),
        cost_estimate=cost(4),
        name="prepare",
    )(in_smem(far_plan), in_hbm(near_field_blocks), in_hbm(coupling.transpose(1, 2, 0)))

    def near_own(plan, blocks):
        return pl.pallas_call(
            near_own_kernel,
            out_shape=acc_shape,
            in_specs=[SMEM, HBM, VMEM],
            out_specs=VMEM,
            scratch_shapes=[
                pltpu.VMEM(panel.shape, f32),
                pltpu.VMEM(low_shape.shape, bf16),
                pltpu.SemaphoreType.DMA,
            ],
            compiler_params=params(),
            cost_estimate=cost(3),
            name="near_own",
        )(in_smem(plan), panel, blocks)

    def near_halves(plan, blocks, kind, same, other, *acc):
        return pl.pallas_call(
            functools.partial(near_halves_kernel, kind),
            out_shape=acc_shape,
            in_specs=[SMEM] + [VMEM] * (3 + len(acc)),
            out_specs=VMEM,
            scratch_shapes=[pltpu.VMEM(low_shape.shape, bf16)],
            compiler_params=params(),
            cost_estimate=cost(2),
            name="near_halves",
        )(in_smem(plan), same, other, blocks, *acc)

    def far(plan, held):
        return pl.pallas_call(
            far_kernel,
            out_shape=(
                jax.ShapeDtypeStruct((clusters, columns, rank), f32),
                jax.ShapeDtypeStruct((half, columns, 2 * rank), bf16),
            ),
            in_specs=[SMEM, VMEM] + [VMEM] * len(held),
            out_specs=(VMEM, VMEM),
            scratch_shapes=[
                pltpu.VMEM((cycle * half, columns, rank), bf16),
                pltpu.VMEM((clusters + 1, columns, rank), f32),
            ],
            compiler_params=params(),
            cost_estimate=cost(3),
            name="far",
        )(in_smem(plan), pairs, *held)

    def finish(plan, blocks, same, other, acc, far_sum, far_other, last):
        outs = (out_shape,) if last else (out_shape, mine_shape, keep_shape, both_shape)
        return pl.pallas_call(
            finish_kernel,
            out_shape=outs,
            in_specs=[SMEM] + [VMEM] * 7,
            out_specs=(VMEM,) * len(outs),
            scratch_shapes=([] if last else [parts])
            + [pltpu.VMEM(acc_shape.shape, f32), pltpu.VMEM(low_shape.shape, bf16)],
            compiler_params=params(),
            cost_estimate=cost(4),
            name="finish",
        )(in_smem(plan), same, other, blocks, acc, far_sum, far_other, basis)

    def other_basis(array):
        return swapped(array, "basis", lambda i: 1 - i)

    def apply_operator(mine, keep, send, near_plan, last):
        paired = swapped(mine, "blk", lambda i: (((i + 1) % cycle ^ 1) - 1) % cycle)
        between = swapped(mine, "blk", lambda i: i ^ 1)
        received = other_basis(send)
        if last:
            acc = near_halves(near_plan, blocks, 0, mine, received)
        else:
            acc = near_own(near_plan, blocks)
        held = [(keep + received[-quarter:].astype(f32)).astype(bf16)]
        held += [swapped(held[0], "blk", lambda i, d=d: i ^ d) for d in range(1, cycle)]
        between, acc, *held = lax.optimization_barrier((between, acc, *held))
        paired_other = other_basis(paired)
        between_other = other_basis(between)
        far_sum, far_send = far(far_plan, held)
        far_other = other_basis(far_send)
        acc = near_halves(near_plan, blocks, 1, paired, paired_other, acc)
        return finish(near_plan, blocks, between, between_other, acc, far_sum, far_other, last), near_plan

    (first, mine, keep, send), near_plan = apply_operator(mine, keep, send, near_plan, False)
    (second,), _ = apply_operator(mine, keep, send, near_plan, True)
    return first.transpose(0, 2, 1), second.transpose(0, 2, 1)


def from_behind(array, axis, by):
    size = lax.axis_size(axis)
    return lax.ppermute(array, axis, [(i, (i + by) % size) for i in range(size)])


def general_on_device(right_panel, near_field_blocks, near_list, cluster_basis, coupling, far_list):
    highest_precision = lax.Precision.HIGHEST
    clusters = right_panel.shape[0]
    slab_rows = cluster_basis.shape[1]
    cycle_place = lax.axis_index("blk")
    cycle_size = lax.axis_size("blk")
    basis_owner = lax.axis_index("basis")
    cluster_ids = jnp.arange(clusters, dtype=jnp.int32)
    near_rows = near_list[:, 0] - cycle_place * clusters
    near_cols = near_list[:, 1]
    row_lookup_table = (near_rows[None, :] == cluster_ids[:, None]).astype(jnp.float32)
    far_table = ((far_list[:, 0] - cycle_place * clusters)[None, :] == cluster_ids[:, None]).astype(
        jnp.float32
    )
    slot_index = (
        near_cols // clusters - cycle_place + 1 + cycle_size
    ) % cycle_size * clusters + near_cols % clusters

    def apply_operator(panel_low):
        own_rows = lax.dynamic_slice_in_dim(panel_low, basis_owner * slab_rows, slab_rows, 1)
        partial_sum = jnp.einsum(
            "nrk,nrc->nkc", cluster_basis, own_rows, preferred_element_type=jnp.float32
        )
        projected = lax.psum(partial_sum, "basis").astype(jnp.bfloat16)
        projections_all = lax.all_gather(projected, "blk", axis=0, tiled=True)
        far_terms = jnp.einsum(
            "pkr,prc->pkc",
            coupling,
            projections_all[far_list[:, 1]],
            preferred_element_type=jnp.float32,
        )
        far_sum = jnp.einsum("np,pkc->nkc", far_table, far_terms, precision=highest_precision)
        far_low = far_sum.astype(jnp.bfloat16)
        pieces = []
        for offset in (1, -1):
            pieces.append(from_behind(panel_low, "blk", offset))
        window = jnp.concatenate([pieces[0], panel_low, pieces[1]], 0)
        source_vector = window[slot_index]
        near_field_products = jnp.einsum(
            "fpz,fzg->fpg", near_field_blocks, source_vector, preferred_element_type=jnp.float32
        )
        near_field_total = jnp.einsum(
            "id,dpb->ipb", row_lookup_table, near_field_products, precision=highest_precision
        )
        far_part = jnp.einsum(
            "nrk,nkc->nrc", cluster_basis, far_low, preferred_element_type=jnp.float32
        )
        return far_part + near_field_total

    krylov_one = apply_operator(right_panel.astype(jnp.bfloat16))
    second_low = lax.all_gather(krylov_one.astype(jnp.bfloat16), "basis", axis=1, tiled=True)
    krylov_two = apply_operator(second_low)
    return (krylov_one, krylov_two)


def on_device(right_panel, near_field_blocks, near_list, cluster_basis, coupling, far_list):
    cycle = lax.axis_size("blk")
    tiled = lax.axis_size("basis") == 2 and cluster_basis.shape[1] % 128 == 0 and cycle & (cycle - 1) == 0
    run = tiled_on_device if tiled else general_on_device
    return run(right_panel, near_field_blocks, near_list, cluster_basis, coupling, far_list)


def solution(mesh):
    placed = (
        P(("groups", "blk"), None, "col"),
        P(("groups", "blk"), "basis", None),
        P(("groups", "blk"), None),
        P(("groups", "blk"), "basis", None),
        P(("groups", "blk"), None, None),
        P(("groups", "blk"), None),
    )
    return jax.shard_map(
        on_device,
        mesh=mesh,
        in_specs=placed,
        out_specs=(P(("groups", "blk"), "basis", "col"), P(("groups", "blk"), "basis", "col")),
        check_vma=False,
    )
```

```python
import functools

import jax
import jax.numpy as jnp
from jax import lax
from jax.experimental import pallas as pl
from jax.experimental.pallas import tpu as pltpu
from jax.sharding import PartitionSpec as P

UNROLL = 16
FIELD = 9
FAR_UNROLL = 32
VMEM = pl.BlockSpec(memory_space=pltpu.VMEM)
ANY = pl.BlockSpec(memory_space=pl.ANY)
HBM = pl.BlockSpec(memory_space=pltpu.HBM)
SMEM = pl.BlockSpec(memory_space=pltpu.SMEM)
TRANSPOSED_RHS = (((1,), (1,)), ((), ()))
PLAIN = (((1,), (0,)), ((), ()))


def swapped(array, axis, partner):
    return lax.ppermute(array, axis, [(i, partner(i)) for i in range(lax.axis_size(axis))])


def dot(a, b, dims):
    return lax.dot_general(a, b, dims, preferred_element_type=jnp.float32)


def params(mebibytes=14):
    return pltpu.CompilerParams(vmem_limit_bytes=mebibytes << 20)


def in_smem(array):
    return pltpu.with_memory_space_constraint(array, pltpu.SMEM)


def in_hbm(array):
    return pltpu.with_memory_space_constraint(array, pltpu.HBM)


def cost(microseconds):
    return pl.CostEstimate(flops=0, transcendentals=0, bytes_accessed=int(microseconds * 3.69e6))


def put_projection(low_ref, basis_ref, keep_ref, send_ref, at, parts):
    quarter = keep_ref.shape[0]
    for part in range(2):
        for n in range(quarter):
            m = 2 * part * quarter + n
            pair = [dot(low_ref[i], basis_ref[i], TRANSPOSED_RHS) for i in (m, m + quarter)]
            parts[part, n] = jnp.concatenate(pair, 1)
    keep_ref[...] = parts[lax.axis_index("basis")]
    send_ref[at:] = parts[1 - lax.axis_index("basis")].astype(jnp.bfloat16)


def start_kernel(panel_hbm, basis_hbm, mine_ref, basis_ref, keep_ref, send_ref, panel, parts, arrived):
    slab = basis_ref.shape[2]
    offset = pl.multiple_of(lax.axis_index("basis") * slab, slab)
    pieces = arrived.shape[0] // 2
    size = panel.shape[0] // pieces
    for i in range(pieces):
        rows = pl.ds(i * size, size)
        pltpu.make_async_copy(panel_hbm.at[rows, :, pl.ds(offset, slab)], panel.at[rows], arrived.at[i]).start()
        pltpu.make_async_copy(basis_hbm.at[rows], basis_ref.at[rows], arrived.at[pieces + i]).start()
    for i in range(pieces):
        rows = pl.ds(i * size, size)
        pltpu.make_async_copy(panel_hbm.at[rows, :, pl.ds(offset, slab)], panel.at[rows], arrived.at[i]).wait()
        mine_ref[rows] = panel[rows].astype(jnp.bfloat16)
    for i in range(pieces):
        rows = pl.ds(i * size, size)
        pltpu.make_async_copy(basis_hbm.at[rows], basis_ref.at[rows], arrived.at[pieces + i]).wait()
    put_projection(mine_ref, basis_ref, keep_ref, send_ref, 0, parts)


def put_sorted(words_ref, kinds, nothing, plan_ref):
    count, width = words_ref.shape[1], plan_ref.shape[1]
    across = jnp.broadcast_to(words_ref[...], (count, count))
    down = across.T
    kind_across, kind_down = lax.shift_right_logical(across, 3 * FIELD), lax.shift_right_logical(down, 3 * FIELD)
    t = lax.broadcasted_iota(jnp.int32, (count, count), 1)
    s = lax.broadcasted_iota(jnp.int32, (count, count), 0)
    before = jnp.sum(((kind_across == kind_down) & (t < s)).astype(jnp.float32), 1, keepdims=True).astype(jnp.int32)
    word = down[:, :1]
    place = lax.broadcasted_iota(jnp.int32, (count, width), 1)
    slot = lax.broadcasted_iota(jnp.int32, (1, width), 1)
    totals = jnp.zeros((1, width), jnp.int32)
    for kind in range(kinds):
        of_kind = kind_down[:, :1] == kind
        total = jnp.sum(of_kind.astype(jnp.float32), 0, keepdims=True).astype(jnp.int32)
        row = jnp.sum(jnp.where(of_kind & (before == place), word, 0), 0, keepdims=True)
        plan_ref[kind : kind + 1] = jnp.where(slot < total, row, nothing)
        totals = jnp.where(slot == kind, total, totals)
    plan_ref[kinds : kinds + 1] = totals


def plan_kernel(nothing, near_ref, far_ref, near_plan_ref, far_plan_ref, near_plan, far_plan, sent):
    put_sorted(near_ref, 3, nothing, near_plan)
    put_sorted(far_ref, 2, nothing, far_plan)
    near_copy = pltpu.make_async_copy(near_plan, near_plan_ref, sent.at[0])
    far_copy = pltpu.make_async_copy(far_plan, far_plan_ref, sent.at[1])
    near_copy.start()
    far_copy.start()
    near_copy.wait()
    far_copy.wait()


def prepare_kernel(far_plan_ref, blocks_hbm, coupling_hbm, blocks_ref, pairs_ref, coupling, turned, arrived):
    pieces = arrived.shape[0] - 1
    size = blocks_ref.shape[0] // pieces
    first = pltpu.make_async_copy(coupling_hbm, coupling, arrived.at[pieces])
    first.start()
    copies = [
        pltpu.make_async_copy(
            blocks_hbm.at[pl.ds(i * size, size)], blocks_ref.at[pl.ds(i * size, size)], arrived.at[i]
        )
        for i in range(pieces)
    ]
    for copy in copies:
        copy.start()
    first.wait()
    rank, _, count = coupling.shape
    for k in range(rank):
        turned[k * count : (k + 1) * count] = coupling[k].astype(jnp.float32).T

    def step(i, carry):
        for j in range(FAR_UNROLL):
            at = i * FAR_UNROLL + j
            pair = lax.shift_right_logical(far_plan_ref[0, at], 2 * FIELD) & ((1 << FIELD) - 1)
            pairs_ref[at] = turned[pl.ds(pair, rank, stride=count)].astype(jnp.bfloat16)
        return carry

    lax.fori_loop(0, lax.div(far_plan_ref[2, 0] + FAR_UNROLL - 1, FAR_UNROLL), step, 0)
    for copy in copies:
        copy.wait()


def add_near(plan_ref, kind, source_ref, blocks_ref, acc_ref):
    mask = (1 << FIELD) - 1

    def step(i, carry):
        words = [plan_ref[kind, i * UNROLL + j] for j in range(UNROLL)]
        terms = []
        for word in words:
            block = blocks_ref[lax.shift_right_logical(word, 2 * FIELD) & mask]
            terms.append(dot(source_ref[word & mask], block, TRANSPOSED_RHS))
        for word, term in zip(words, terms):
            row = lax.shift_right_logical(word, FIELD) & mask
            acc_ref[row] = acc_ref[row] + term
        return carry

    lax.fori_loop(0, lax.div(plan_ref[3, kind] + UNROLL - 1, UNROLL), step, 0)


def near_own_kernel(plan_ref, panel_hbm, blocks_ref, acc_ref, panel, low, arrived):
    copy = pltpu.make_async_copy(panel_hbm, panel, arrived)
    copy.start()
    acc_ref[...] = jnp.zeros_like(acc_ref)
    copy.wait()
    low[...] = panel[...].astype(jnp.bfloat16)
    add_near(plan_ref, 0, low, blocks_ref, acc_ref)


def put_whole(same_ref, other_ref, whole):
    slab = same_ref.shape[2]
    first = lax.axis_index("basis") == 0
    same, other = same_ref[...], other_ref[: same_ref.shape[0]]
    whole[:, :, :slab] = jnp.where(first, same, other)
    whole[:, :, slab:] = jnp.where(first, other, same)


def near_halves_kernel(kind, plan_ref, same_ref, other_ref, blocks_ref, *refs):
    acc_ref, whole = refs[-2:]
    put_whole(same_ref, other_ref, whole)
    acc_ref[...] = refs[0][...] if len(refs) == 3 else jnp.zeros_like(acc_ref)
    add_near(plan_ref, kind, whole, blocks_ref, acc_ref)


def far_kernel(plan_ref, pairs_ref, *refs):
    held, keep_ref, send_ref, unpacked, acc = refs[:-4], *refs[-4:]
    clusters = keep_ref.shape[0]
    quarter = held[0].shape[0]
    rank = pairs_ref.shape[1]
    mask = (1 << FIELD) - 1
    for d, packed in enumerate(held):
        unpacked[2 * d * quarter : (2 * d + 1) * quarter] = packed[:, :, :rank]
        unpacked[(2 * d + 1) * quarter : (2 * d + 2) * quarter] = packed[:, :, rank:]
    acc[...] = jnp.zeros_like(acc)

    def step(i, carry):
        words = [plan_ref[0, i * FAR_UNROLL + j] for j in range(FAR_UNROLL)]
        terms = []
        for j, word in enumerate(words):
            terms.append(dot(unpacked[word & mask], pairs_ref[i * FAR_UNROLL + j], TRANSPOSED_RHS))
        for word, term in zip(words, terms):
            row = lax.shift_right_logical(word, FIELD) & mask
            acc[row] = acc[row] + term
        return carry

    lax.fori_loop(0, lax.div(plan_ref[2, 0] + FAR_UNROLL - 1, FAR_UNROLL), step, 0)
    half = clusters // 2
    for n in range(half):
        keep_ref[n] = acc[n]
        keep_ref[n + half] = acc[n + half]
        send_ref[n] = jnp.concatenate([acc[n], acc[n + half]], 1).astype(jnp.bfloat16)


def finish_kernel(plan_ref, same_ref, other_ref, blocks_ref, acc_in, far_ref, far_other_ref, basis_ref, *refs):
    out_hbm, (acc_ref, whole, out_ref, sent) = refs[0], refs[-4:]
    near_halves_kernel(2, plan_ref, same_ref, other_ref, blocks_ref, acc_in, acc_ref, whole)
    half, _, wide = far_other_ref.shape
    rank = wide // 2
    pieces = sent.shape[0]
    size = 2 * half // pieces
    copies = []
    for n in range(2 * half):
        other = far_other_ref[n, :, :rank] if n < half else far_other_ref[n - half, :, rank:]
        far_low = (far_ref[n] + other.astype(jnp.float32)).astype(jnp.bfloat16)
        out_ref[n] = acc_ref[n] + dot(far_low, basis_ref[n], PLAIN)
        if (n + 1) % size == 0:
            rows = pl.ds(n + 1 - size, size)
            copies.append(pltpu.make_async_copy(out_ref.at[rows], out_hbm.at[rows], sent.at[n // size]))
            copies[-1].start()
    if len(refs) == 9:
        mine_ref, keep_ref, send_ref, parts = refs[1:5]
        low = out_ref[...].astype(jnp.bfloat16)
        mine_ref[...] = low
        send_ref[: 2 * half] = low
        put_projection(mine_ref, basis_ref, keep_ref, send_ref, 2 * half, parts)
    for copy in copies:
        copy.wait()


def tiled_on_device(right_panel, near_field_blocks, near_list, cluster_basis, coupling, far_list):
    clusters, points, columns = right_panel.shape
    near_count = near_list.shape[0]
    slab, rank = cluster_basis.shape[1:]
    panel = right_panel.transpose(0, 2, 1)
    basis = cluster_basis.transpose(0, 2, 1)
    cycle = lax.axis_size("blk")
    place = jnp.stack([lax.axis_index("blk"), lax.axis_index("basis")]).astype(jnp.int32)
    half, quarter = clusters // 2, clusters // 4
    near_owner, far_owner = near_list[:, 1] // clusters, far_list[:, 1] // clusters
    words = jnp.where(near_owner == place[0], 0, jnp.where(near_owner == place[0] ^ 1, 2, 1))
    words = words << FIELD | jnp.arange(near_count, dtype=jnp.int32)
    words = words << FIELD | near_list[:, 0] - place[0] * clusters
    words = words << FIELD | near_list[:, 1] % clusters
    far_source = far_list[:, 1] % clusters
    far_words = (far_source // half != place[1]).astype(jnp.int32)
    far_words = far_words << FIELD | jnp.arange(far_list.shape[0], dtype=jnp.int32)
    far_words = far_words << FIELD | far_list[:, 0] - place[0] * clusters
    far_words = far_words << FIELD | (place[0] ^ far_owner) * half + far_source % half
    f32, bf16 = jnp.float32, jnp.bfloat16
    mine_shape = jax.ShapeDtypeStruct((clusters, columns, slab), bf16)
    keep_shape = jax.ShapeDtypeStruct((quarter, columns, 2 * rank), f32)
    send_shape = jax.ShapeDtypeStruct((quarter, columns, 2 * rank), bf16)
    both_shape = jax.ShapeDtypeStruct((clusters + quarter, columns, slab), bf16)
    parts = pltpu.VMEM((2, quarter, columns, 2 * rank), f32)
    out_shape = jax.ShapeDtypeStruct((clusters, columns, slab), f32)
    acc_shape = jax.ShapeDtypeStruct((clusters + 1, columns, slab), f32)
    near_plan_shape = jax.ShapeDtypeStruct((4, near_count + UNROLL), jnp.int32)
    far_plan_shape = jax.ShapeDtypeStruct((3, far_list.shape[0] + FAR_UNROLL), jnp.int32)

    low_shape = jax.ShapeDtypeStruct((clusters, columns, points), bf16)
    pieces = 4
    mine, basis, keep, send = pl.pallas_call(
        start_kernel,
        out_shape=(mine_shape, jax.ShapeDtypeStruct(basis.shape, bf16), keep_shape, send_shape),
        in_specs=[HBM, HBM],
        out_specs=(VMEM,) * 4,
        scratch_shapes=[pltpu.VMEM(mine_shape.shape, f32), parts, pltpu.SemaphoreType.DMA((2 * pieces,))],
        compiler_params=params(),
        cost_estimate=cost(2),
        name="start",
    )(in_hbm(panel), in_hbm(basis))
    near_plan, far_plan = pl.pallas_call(
        functools.partial(plan_kernel, clusters << FIELD),
        out_shape=(
            pltpu.SMEM(near_plan_shape.shape, jnp.int32),
            pltpu.SMEM(far_plan_shape.shape, jnp.int32),
        ),
        in_specs=[VMEM, VMEM],
        out_specs=(SMEM, SMEM),
        scratch_shapes=[
            pltpu.VMEM(near_plan_shape.shape, jnp.int32),
            pltpu.VMEM(far_plan_shape.shape, jnp.int32),
            pltpu.SemaphoreType.DMA((2,)),
        ],
        compiler_params=params(),
        cost_estimate=cost(1),
        name="plan",
    )(words[None], far_words[None])
    blocks, pairs = pl.pallas_call(
        prepare_kernel,
        out_shape=(
            pltpu.VMEM(near_field_blocks.shape, bf16),
            pltpu.VMEM((coupling.shape[0] + FAR_UNROLL, rank, rank), bf16),
        ),
        in_specs=[SMEM, HBM, HBM],
        out_specs=(VMEM, VMEM),
        scratch_shapes=[
            pltpu.VMEM((rank, rank, coupling.shape[0]), bf16),
            pltpu.VMEM((rank * coupling.shape[0], rank), f32),
            pltpu.SemaphoreType.DMA((9,)),
        ],
        compiler_params=params(20),
        cost_estimate=cost(4),
        name="prepare",
    )(in_smem(far_plan), in_hbm(near_field_blocks), in_hbm(coupling.transpose(1, 2, 0)))

    def near_own(plan, blocks):
        return pl.pallas_call(
            near_own_kernel,
            out_shape=acc_shape,
            in_specs=[SMEM, HBM, VMEM],
            out_specs=VMEM,
            scratch_shapes=[
                pltpu.VMEM(panel.shape, f32),
                pltpu.VMEM(low_shape.shape, bf16),
                pltpu.SemaphoreType.DMA,
            ],
            compiler_params=params(),
            cost_estimate=cost(3),
            name="near_own",
        )(in_smem(plan), panel, blocks)

    def near_halves(plan, blocks, kind, same, other, *acc):
        return pl.pallas_call(
            functools.partial(near_halves_kernel, kind),
            out_shape=acc_shape,
            in_specs=[SMEM] + [VMEM] * (3 + len(acc)),
            out_specs=VMEM,
            scratch_shapes=[pltpu.VMEM(low_shape.shape, bf16)],
            compiler_params=params(),
            cost_estimate=cost(2),
            name="near_halves",
        )(in_smem(plan), same, other, blocks, *acc)

    def far(plan, held):
        return pl.pallas_call(
            far_kernel,
            out_shape=(
                jax.ShapeDtypeStruct((clusters, columns, rank), f32),
                jax.ShapeDtypeStruct((half, columns, 2 * rank), bf16),
            ),
            in_specs=[SMEM, VMEM] + [VMEM] * len(held),
            out_specs=(VMEM, VMEM),
            scratch_shapes=[
                pltpu.VMEM((cycle * half, columns, rank), bf16),
                pltpu.VMEM((clusters + 1, columns, rank), f32),
            ],
            compiler_params=params(),
            cost_estimate=cost(3),
            name="far",
        )(in_smem(plan), pairs, *held)

    def finish(plan, blocks, same, other, acc, far_sum, far_other, last):
        outs = (out_shape,) if last else (out_shape, mine_shape, keep_shape, both_shape)
        return pl.pallas_call(
            finish_kernel,
            out_shape=outs,
            in_specs=[SMEM] + [VMEM] * 7,
            out_specs=(HBM,) + (VMEM,) * (len(outs) - 1),
            scratch_shapes=([] if last else [parts])
            + [pltpu.VMEM(acc_shape.shape, f32), pltpu.VMEM(low_shape.shape, bf16)]
            + [pltpu.VMEM(out_shape.shape, f32), pltpu.SemaphoreType.DMA((4,))],
            compiler_params=params(),
            cost_estimate=cost(4),
            name="finish",
        )(in_smem(plan), same, other, blocks, acc, far_sum, far_other, basis)

    def other_basis(array):
        return swapped(array, "basis", lambda i: 1 - i)

    def apply_operator(mine, keep, send, near_plan, last):
        paired = swapped(mine, "blk", lambda i: (((i + 1) % cycle ^ 1) - 1) % cycle)
        between = swapped(mine, "blk", lambda i: i ^ 1)
        received = other_basis(send)
        if last:
            acc = near_halves(near_plan, blocks, 0, mine, received)
        else:
            acc = near_own(near_plan, blocks)
        held = [(keep + received[-quarter:].astype(f32)).astype(bf16)]
        held += [swapped(held[0], "blk", lambda i, d=d: i ^ d) for d in range(1, cycle)]
        between, acc, *held = lax.optimization_barrier((between, acc, *held))
        paired_other = other_basis(paired)
        between_other = other_basis(between)
        far_sum, far_send = far(far_plan, held)
        far_other = other_basis(far_send)
        acc = near_halves(near_plan, blocks, 1, paired, paired_other, acc)
        return finish(near_plan, blocks, between, between_other, acc, far_sum, far_other, last), near_plan

    (first, mine, keep, send), near_plan = apply_operator(mine, keep, send, near_plan, False)
    (second,), _ = apply_operator(mine, keep, send, near_plan, True)
    return first.transpose(0, 2, 1), second.transpose(0, 2, 1)


def from_behind(array, axis, by):
    size = lax.axis_size(axis)
    return lax.ppermute(array, axis, [(i, (i + by) % size) for i in range(size)])


def general_on_device(right_panel, near_field_blocks, near_list, cluster_basis, coupling, far_list):
    highest_precision = lax.Precision.HIGHEST
    clusters = right_panel.shape[0]
    slab_rows = cluster_basis.shape[1]
    cycle_place = lax.axis_index("blk")
    cycle_size = lax.axis_size("blk")
    basis_owner = lax.axis_index("basis")
    cluster_ids = jnp.arange(clusters, dtype=jnp.int32)
    near_rows = near_list[:, 0] - cycle_place * clusters
    near_cols = near_list[:, 1]
    row_lookup_table = (near_rows[None, :] == cluster_ids[:, None]).astype(jnp.float32)
    far_table = ((far_list[:, 0] - cycle_place * clusters)[None, :] == cluster_ids[:, None]).astype(
        jnp.float32
    )
    slot_index = (
        near_cols // clusters - cycle_place + 1 + cycle_size
    ) % cycle_size * clusters + near_cols % clusters

    def apply_operator(panel_low):
        own_rows = lax.dynamic_slice_in_dim(panel_low, basis_owner * slab_rows, slab_rows, 1)
        partial_sum = jnp.einsum(
            "nrk,nrc->nkc", cluster_basis, own_rows, preferred_element_type=jnp.float32
        )
        projected = lax.psum(partial_sum, "basis").astype(jnp.bfloat16)
        projections_all = lax.all_gather(projected, "blk", axis=0, tiled=True)
        far_terms = jnp.einsum(
            "pkr,prc->pkc",
            coupling,
            projections_all[far_list[:, 1]],
            preferred_element_type=jnp.float32,
        )
        far_sum = jnp.einsum("np,pkc->nkc", far_table, far_terms, precision=highest_precision)
        far_low = far_sum.astype(jnp.bfloat16)
        pieces = []
        for offset in (1, -1):
            pieces.append(from_behind(panel_low, "blk", offset))
        window = jnp.concatenate([pieces[0], panel_low, pieces[1]], 0)
        source_vector = window[slot_index]
        near_field_products = jnp.einsum(
            "fpz,fzg->fpg", near_field_blocks, source_vector, preferred_element_type=jnp.float32
        )
        near_field_total = jnp.einsum(
            "id,dpb->ipb", row_lookup_table, near_field_products, precision=highest_precision
        )
        far_part = jnp.einsum(
            "nrk,nkc->nrc", cluster_basis, far_low, preferred_element_type=jnp.float32
        )
        return far_part + near_field_total

    krylov_one = apply_operator(right_panel.astype(jnp.bfloat16))
    second_low = lax.all_gather(krylov_one.astype(jnp.bfloat16), "basis", axis=1, tiled=True)
    krylov_two = apply_operator(second_low)
    return (krylov_one, krylov_two)


def on_device(right_panel, near_field_blocks, near_list, cluster_basis, coupling, far_list):
    cycle = lax.axis_size("blk")
    tiled = lax.axis_size("basis") == 2 and cluster_basis.shape[1] % 128 == 0 and cycle & (cycle - 1) == 0
    run = tiled_on_device if tiled else general_on_device
    return run(right_panel, near_field_blocks, near_list, cluster_basis, coupling, far_list)


def solution(mesh):
    placed = (
        P(("groups", "blk"), None, "col"),
        P(("groups", "blk"), "basis", None),
        P(("groups", "blk"), None),
        P(("groups", "blk"), "basis", None),
        P(("groups", "blk"), None, None),
        P(("groups", "blk"), None),
    )
    return jax.shard_map(
        on_device,
        mesh=mesh,
        in_specs=placed,
        out_specs=(P(("groups", "blk"), "basis", "col"), P(("groups", "blk"), "basis", "col")),
        check_vma=False,
    )
```

```python
import functools

import jax
import jax.numpy as jnp
from jax import lax
from jax.experimental import pallas as pl
from jax.experimental.pallas import tpu as pltpu
from jax.sharding import PartitionSpec as P

UNROLL = 16
FIELD = 9
FAR_UNROLL = 32
VMEM = pl.BlockSpec(memory_space=pltpu.VMEM)
ANY = pl.BlockSpec(memory_space=pl.ANY)
HBM = pl.BlockSpec(memory_space=pltpu.HBM)
SMEM = pl.BlockSpec(memory_space=pltpu.SMEM)
TRANSPOSED_RHS = (((1,), (1,)), ((), ()))
PLAIN = (((1,), (0,)), ((), ()))


def swapped(array, axis, partner):
    return lax.ppermute(array, axis, [(i, partner(i)) for i in range(lax.axis_size(axis))])


def dot(a, b, dims):
    return lax.dot_general(a, b, dims, preferred_element_type=jnp.float32)


def params(mebibytes=14):
    return pltpu.CompilerParams(vmem_limit_bytes=mebibytes << 20)


def in_smem(array):
    return pltpu.with_memory_space_constraint(array, pltpu.SMEM)


def in_hbm(array):
    return pltpu.with_memory_space_constraint(array, pltpu.HBM)


def cost(microseconds):
    return pl.CostEstimate(flops=0, transcendentals=0, bytes_accessed=int(microseconds * 3.69e6))


def put_projection(low_ref, basis_ref, keep_ref, send_ref, at, parts):
    quarter = keep_ref.shape[0]
    for part in range(2):
        for n in range(quarter):
            m = 2 * part * quarter + n
            pair = [dot(low_ref[i], basis_ref[i], TRANSPOSED_RHS) for i in (m, m + quarter)]
            parts[part, n] = jnp.concatenate(pair, 1)
    keep_ref[...] = parts[lax.axis_index("basis")]
    send_ref[at:] = parts[1 - lax.axis_index("basis")].astype(jnp.bfloat16)


def start_kernel(panel_hbm, basis_hbm, mine_ref, basis_ref, keep_ref, send_ref, panel, parts, arrived):
    slab = basis_ref.shape[2]
    offset = pl.multiple_of(lax.axis_index("basis") * slab, slab)
    pieces = arrived.shape[0] // 2
    size = panel.shape[0] // pieces
    for i in range(pieces):
        rows = pl.ds(i * size, size)
        pltpu.make_async_copy(panel_hbm.at[rows, :, pl.ds(offset, slab)], panel.at[rows], arrived.at[i]).start()
        pltpu.make_async_copy(basis_hbm.at[rows], basis_ref.at[rows], arrived.at[pieces + i]).start()
    for i in range(pieces):
        rows = pl.ds(i * size, size)
        pltpu.make_async_copy(panel_hbm.at[rows, :, pl.ds(offset, slab)], panel.at[rows], arrived.at[i]).wait()
        mine_ref[rows] = panel[rows].astype(jnp.bfloat16)
    for i in range(pieces):
        rows = pl.ds(i * size, size)
        pltpu.make_async_copy(basis_hbm.at[rows], basis_ref.at[rows], arrived.at[pieces + i]).wait()
    put_projection(mine_ref, basis_ref, keep_ref, send_ref, 0, parts)


def put_sorted(words, kinds, nothing, plan_ref):
    count, width = words.shape[1], plan_ref.shape[1]
    across = jnp.broadcast_to(words, (count, count))
    down = across.T
    kind_across, kind_down = lax.shift_right_logical(across, 3 * FIELD), lax.shift_right_logical(down, 3 * FIELD)
    t = lax.broadcasted_iota(jnp.int32, (count, count), 1)
    s = lax.broadcasted_iota(jnp.int32, (count, count), 0)
    before = jnp.sum(((kind_across == kind_down) & (t < s)).astype(jnp.float32), 1, keepdims=True).astype(jnp.int32)
    word = down[:, :1]
    place = lax.broadcasted_iota(jnp.int32, (count, width), 1)
    slot = lax.broadcasted_iota(jnp.int32, (1, width), 1)
    totals = jnp.zeros((1, width), jnp.int32)
    for kind in range(kinds):
        of_kind = kind_down[:, :1] == kind
        total = jnp.sum(of_kind.astype(jnp.float32), 0, keepdims=True).astype(jnp.int32)
        row = jnp.sum(jnp.where(of_kind & (before == place), word, 0), 0, keepdims=True)
        plan_ref[kind : kind + 1] = jnp.where(slot < total, row, nothing)
        totals = jnp.where(slot == kind, total, totals)
    plan_ref[kinds : kinds + 1] = totals


def put_plans(clusters, near_ref, far_ref, near_plan, far_plan):
    here, basis = lax.axis_index("blk"), lax.axis_index("basis")
    bits, half = clusters.bit_length() - 1, clusters // 2
    rows, columns = near_ref[0:1], near_ref[1:2]
    entry = lax.broadcasted_iota(jnp.int32, rows.shape, 1)
    owner = lax.shift_right_logical(columns, bits)
    kind = jnp.where(owner == here, 0, jnp.where(owner == (here ^ 1), 2, 1))
    words = ((kind << FIELD | entry) << FIELD | (rows - here * clusters)) << FIELD | (columns & (clusters - 1))
    put_sorted(words, 3, clusters << FIELD, near_plan)
    rows, columns = far_ref[0:1], far_ref[1:2]
    entry = lax.broadcasted_iota(jnp.int32, rows.shape, 1)
    owner, source = lax.shift_right_logical(columns, bits), columns & (clusters - 1)
    kind = jnp.where(lax.shift_right_logical(source, bits - 1) == basis, 0, 1)
    place = (owner ^ here) * half + (source & (half - 1))
    words = ((kind << FIELD | entry) << FIELD | (rows - here * clusters)) << FIELD | place
    put_sorted(words, 2, clusters << FIELD, far_plan)


def prepare_kernel(clusters, near_hbm, far_hbm, blocks_hbm, coupling_hbm, *refs):
    near_plan_ref, far_plan_ref, blocks_ref, pairs_ref, coupling, turned, near_plan, far_plan, lists, arrived = refs

    def copies_of(source, target, pieces, first):
        size = target.shape[0] // pieces
        parts = [pl.ds(i * size, size) for i in range(pieces)]
        return [
            pltpu.make_async_copy(source.at[part], target.at[part], arrived.at[first + i])
            for i, part in enumerate(parts)
        ]

    coupling_copies = copies_of(coupling_hbm, coupling, 4, 0)
    block_copies = copies_of(blocks_hbm, blocks_ref, 8, 4)
    list_copies = [
        pltpu.make_async_copy(source, lists.at[i], arrived.at[14 + i]) for i, source in enumerate((near_hbm, far_hbm))
    ]
    for copy in list_copies + coupling_copies + block_copies:
        copy.start()
    for copy in list_copies:
        copy.wait()
    put_plans(clusters, lists.at[0], lists.at[1], near_plan, far_plan)
    plan_copies = [
        pltpu.make_async_copy(near_plan, near_plan_ref, arrived.at[12]),
        pltpu.make_async_copy(far_plan, far_plan_ref, arrived.at[13]),
    ]
    for copy in plan_copies:
        copy.start()
    rank, _, count = coupling.shape
    for copy in coupling_copies:
        copy.wait()
    for k in range(rank):
        turned[k * count : (k + 1) * count] = coupling[k].astype(jnp.float32).T
    for copy in plan_copies:
        copy.wait()

    def step(i, carry):
        for j in range(FAR_UNROLL):
            at = i * FAR_UNROLL + j
            pair = lax.shift_right_logical(far_plan_ref[0, at], 2 * FIELD) & ((1 << FIELD) - 1)
            pairs_ref[at] = turned[pl.ds(pair, rank, stride=count)].astype(jnp.bfloat16)
        return carry

    lax.fori_loop(0, lax.div(far_plan_ref[2, 0] + FAR_UNROLL - 1, FAR_UNROLL), step, 0)
    for copy in block_copies:
        copy.wait()


def add_near(plan_ref, kind, source_ref, blocks_ref, acc_ref):
    mask = (1 << FIELD) - 1

    def step(i, carry):
        words = [plan_ref[kind, i * UNROLL + j] for j in range(UNROLL)]
        terms = []
        for word in words:
            block = blocks_ref[lax.shift_right_logical(word, 2 * FIELD) & mask]
            terms.append(dot(source_ref[word & mask], block, TRANSPOSED_RHS))
        for word, term in zip(words, terms):
            row = lax.shift_right_logical(word, FIELD) & mask
            acc_ref[row] = acc_ref[row] + term
        return carry

    lax.fori_loop(0, lax.div(plan_ref[3, kind] + UNROLL - 1, UNROLL), step, 0)


def near_own_kernel(plan_ref, panel_hbm, blocks_ref, acc_ref, panel, low, arrived):
    copy = pltpu.make_async_copy(panel_hbm, panel, arrived)
    copy.start()
    acc_ref[...] = jnp.zeros_like(acc_ref)
    copy.wait()
    low[...] = panel[...].astype(jnp.bfloat16)
    add_near(plan_ref, 0, low, blocks_ref, acc_ref)


def put_whole(same_ref, other_ref, whole):
    slab = same_ref.shape[2]
    first = lax.axis_index("basis") == 0
    same, other = same_ref[...], other_ref[: same_ref.shape[0]]
    whole[:, :, :slab] = jnp.where(first, same, other)
    whole[:, :, slab:] = jnp.where(first, other, same)


def near_halves_kernel(kind, plan_ref, same_ref, other_ref, blocks_ref, *refs):
    acc_ref, whole = refs[-2:]
    put_whole(same_ref, other_ref, whole)
    acc_ref[...] = refs[0][...] if len(refs) == 3 else jnp.zeros_like(acc_ref)
    add_near(plan_ref, kind, whole, blocks_ref, acc_ref)


def far_kernel(plan_ref, pairs_ref, *refs):
    held, keep_ref, send_ref, unpacked, acc = refs[:-4], *refs[-4:]
    clusters = keep_ref.shape[0]
    quarter = held[0].shape[0]
    rank = pairs_ref.shape[1]
    mask = (1 << FIELD) - 1
    for d, packed in enumerate(held):
        unpacked[2 * d * quarter : (2 * d + 1) * quarter] = packed[:, :, :rank]
        unpacked[(2 * d + 1) * quarter : (2 * d + 2) * quarter] = packed[:, :, rank:]
    acc[...] = jnp.zeros_like(acc)

    def step(i, carry):
        words = [plan_ref[0, i * FAR_UNROLL + j] for j in range(FAR_UNROLL)]
        terms = []
        for j, word in enumerate(words):
            terms.append(dot(unpacked[word & mask], pairs_ref[i * FAR_UNROLL + j], TRANSPOSED_RHS))
        for word, term in zip(words, terms):
            row = lax.shift_right_logical(word, FIELD) & mask
            acc[row] = acc[row] + term
        return carry

    lax.fori_loop(0, lax.div(plan_ref[2, 0] + FAR_UNROLL - 1, FAR_UNROLL), step, 0)
    half = clusters // 2
    for n in range(half):
        keep_ref[n] = acc[n]
        keep_ref[n + half] = acc[n + half]
        send_ref[n] = jnp.concatenate([acc[n], acc[n + half]], 1).astype(jnp.bfloat16)


def finish_kernel(plan_ref, same_ref, other_ref, blocks_ref, acc_in, far_ref, far_other_ref, basis_ref, *refs):
    out_hbm, (acc_ref, whole, out_ref, sent) = refs[0], refs[-4:]
    near_halves_kernel(2, plan_ref, same_ref, other_ref, blocks_ref, acc_in, acc_ref, whole)
    half, _, wide = far_other_ref.shape
    rank = wide // 2
    pieces = sent.shape[0]
    size = 2 * half // pieces
    copies = []
    for n in range(2 * half):
        other = far_other_ref[n, :, :rank] if n < half else far_other_ref[n - half, :, rank:]
        far_low = (far_ref[n] + other.astype(jnp.float32)).astype(jnp.bfloat16)
        out_ref[n] = acc_ref[n] + dot(far_low, basis_ref[n], PLAIN)
        if (n + 1) % size == 0:
            rows = pl.ds(n + 1 - size, size)
            copies.append(pltpu.make_async_copy(out_ref.at[rows], out_hbm.at[rows], sent.at[n // size]))
            copies[-1].start()
    if len(refs) == 9:
        mine_ref, keep_ref, send_ref, parts = refs[1:5]
        low = out_ref[...].astype(jnp.bfloat16)
        mine_ref[...] = low
        send_ref[: 2 * half] = low
        put_projection(mine_ref, basis_ref, keep_ref, send_ref, 2 * half, parts)
    for copy in copies:
        copy.wait()


def tiled_on_device(right_panel, near_field_blocks, near_list, cluster_basis, coupling, far_list):
    clusters, points, columns = right_panel.shape
    near_count = near_list.shape[0]
    slab, rank = cluster_basis.shape[1:]
    panel = right_panel.transpose(0, 2, 1)
    basis = cluster_basis.transpose(0, 2, 1)
    cycle = lax.axis_size("blk")
    half, quarter = clusters // 2, clusters // 4
    f32, bf16 = jnp.float32, jnp.bfloat16
    mine_shape = jax.ShapeDtypeStruct((clusters, columns, slab), bf16)
    keep_shape = jax.ShapeDtypeStruct((quarter, columns, 2 * rank), f32)
    send_shape = jax.ShapeDtypeStruct((quarter, columns, 2 * rank), bf16)
    both_shape = jax.ShapeDtypeStruct((clusters + quarter, columns, slab), bf16)
    parts = pltpu.VMEM((2, quarter, columns, 2 * rank), f32)
    out_shape = jax.ShapeDtypeStruct((clusters, columns, slab), f32)
    acc_shape = jax.ShapeDtypeStruct((clusters + 1, columns, slab), f32)
    near_plan_shape = jax.ShapeDtypeStruct((4, near_count + UNROLL), jnp.int32)
    far_plan_shape = jax.ShapeDtypeStruct((3, far_list.shape[0] + FAR_UNROLL), jnp.int32)

    low_shape = jax.ShapeDtypeStruct((clusters, columns, points), bf16)
    pieces = 4
    mine, basis, keep, send = pl.pallas_call(
        start_kernel,
        out_shape=(mine_shape, jax.ShapeDtypeStruct(basis.shape, bf16), keep_shape, send_shape),
        in_specs=[HBM, HBM],
        out_specs=(VMEM,) * 4,
        scratch_shapes=[pltpu.VMEM(mine_shape.shape, f32), parts, pltpu.SemaphoreType.DMA((2 * pieces,))],
        compiler_params=params(),
        cost_estimate=cost(2),
        name="start",
    )(in_hbm(panel), in_hbm(basis))
    near_plan, far_plan, blocks, pairs = pl.pallas_call(
        functools.partial(prepare_kernel, clusters),
        out_shape=(
            pltpu.SMEM(near_plan_shape.shape, jnp.int32),
            pltpu.SMEM(far_plan_shape.shape, jnp.int32),
            pltpu.VMEM(near_field_blocks.shape, bf16),
            pltpu.VMEM((coupling.shape[0] + FAR_UNROLL, rank, rank), bf16),
        ),
        in_specs=[HBM] * 4,
        out_specs=(SMEM, SMEM, VMEM, VMEM),
        scratch_shapes=[
            pltpu.VMEM((rank, rank, coupling.shape[0]), bf16),
            pltpu.VMEM(((rank + 1) * coupling.shape[0], rank), f32),
            pltpu.VMEM(near_plan_shape.shape, jnp.int32),
            pltpu.VMEM(far_plan_shape.shape, jnp.int32),
            pltpu.VMEM((2, 2, near_count), jnp.int32),
            pltpu.SemaphoreType.DMA((16,)),
        ],
        compiler_params=params(20),
        cost_estimate=cost(4),
        name="prepare",
    )(*(in_hbm(array) for array in (near_list.T, far_list.T, near_field_blocks, coupling.transpose(1, 2, 0))))

    def near_own(plan, blocks):
        return pl.pallas_call(
            near_own_kernel,
            out_shape=acc_shape,
            in_specs=[SMEM, HBM, VMEM],
            out_specs=VMEM,
            scratch_shapes=[
                pltpu.VMEM(panel.shape, f32),
                pltpu.VMEM(low_shape.shape, bf16),
                pltpu.SemaphoreType.DMA,
            ],
            compiler_params=params(),
            cost_estimate=cost(3),
            name="near_own",
        )(in_smem(plan), panel, blocks)

    def near_halves(plan, blocks, kind, same, other, *acc):
        return pl.pallas_call(
            functools.partial(near_halves_kernel, kind),
            out_shape=acc_shape,
            in_specs=[SMEM] + [VMEM] * (3 + len(acc)),
            out_specs=VMEM,
            scratch_shapes=[pltpu.VMEM(low_shape.shape, bf16)],
            compiler_params=params(),
            cost_estimate=cost(2),
            name="near_halves",
        )(in_smem(plan), same, other, blocks, *acc)

    def far(plan, held):
        return pl.pallas_call(
            far_kernel,
            out_shape=(
                jax.ShapeDtypeStruct((clusters, columns, rank), f32),
                jax.ShapeDtypeStruct((half, columns, 2 * rank), bf16),
            ),
            in_specs=[SMEM, VMEM] + [VMEM] * len(held),
            out_specs=(VMEM, VMEM),
            scratch_shapes=[
                pltpu.VMEM((cycle * half, columns, rank), bf16),
                pltpu.VMEM((clusters + 1, columns, rank), f32),
            ],
            compiler_params=params(),
            cost_estimate=cost(3),
            name="far",
        )(in_smem(plan), pairs, *held)

    def finish(plan, blocks, same, other, acc, far_sum, far_other, last):
        outs = (out_shape,) if last else (out_shape, mine_shape, keep_shape, both_shape)
        return pl.pallas_call(
            finish_kernel,
            out_shape=outs,
            in_specs=[SMEM] + [VMEM] * 7,
            out_specs=(HBM,) + (VMEM,) * (len(outs) - 1),
            scratch_shapes=([] if last else [parts])
            + [pltpu.VMEM(acc_shape.shape, f32), pltpu.VMEM(low_shape.shape, bf16)]
            + [pltpu.VMEM(out_shape.shape, f32), pltpu.SemaphoreType.DMA((4,))],
            compiler_params=params(),
            cost_estimate=cost(4),
            name="finish",
        )(in_smem(plan), same, other, blocks, acc, far_sum, far_other, basis)

    def other_basis(array):
        return swapped(array, "basis", lambda i: 1 - i)

    def apply_operator(mine, keep, send, near_plan, last):
        paired = swapped(mine, "blk", lambda i: (((i + 1) % cycle ^ 1) - 1) % cycle)
        between = swapped(mine, "blk", lambda i: i ^ 1)
        received = other_basis(send)
        if last:
            acc = near_halves(near_plan, blocks, 0, mine, received)
        else:
            acc = near_own(near_plan, blocks)
        held = [(keep + received[-quarter:].astype(f32)).astype(bf16)]
        got = {0: held[0]}
        for d in reversed([1 << i for i in range(cycle.bit_length() - 1)]):
            for e in list(got):
                got[e ^ d] = swapped(got[e], "blk", lambda i, d=d: i ^ d)
        held = [got[d] for d in range(cycle)]
        between, acc, held[1], held[2] = lax.optimization_barrier((between, acc, held[1], held[2]))
        paired_other = other_basis(paired)
        between_other = other_basis(between)
        far_sum, far_send = far(far_plan, held)
        far_other = other_basis(far_send)
        acc = near_halves(near_plan, blocks, 1, paired, paired_other, acc)
        return finish(near_plan, blocks, between, between_other, acc, far_sum, far_other, last), near_plan

    (first, mine, keep, send), near_plan = apply_operator(mine, keep, send, near_plan, False)
    (second,), _ = apply_operator(mine, keep, send, near_plan, True)
    return first.transpose(0, 2, 1), second.transpose(0, 2, 1)


def from_behind(array, axis, by):
    size = lax.axis_size(axis)
    return lax.ppermute(array, axis, [(i, (i + by) % size) for i in range(size)])


def general_on_device(right_panel, near_field_blocks, near_list, cluster_basis, coupling, far_list):
    highest_precision = lax.Precision.HIGHEST
    clusters = right_panel.shape[0]
    slab_rows = cluster_basis.shape[1]
    cycle_place = lax.axis_index("blk")
    cycle_size = lax.axis_size("blk")
    basis_owner = lax.axis_index("basis")
    cluster_ids = jnp.arange(clusters, dtype=jnp.int32)
    near_rows = near_list[:, 0] - cycle_place * clusters
    near_cols = near_list[:, 1]
    row_lookup_table = (near_rows[None, :] == cluster_ids[:, None]).astype(jnp.float32)
    far_table = ((far_list[:, 0] - cycle_place * clusters)[None, :] == cluster_ids[:, None]).astype(
        jnp.float32
    )
    slot_index = (
        near_cols // clusters - cycle_place + 1 + cycle_size
    ) % cycle_size * clusters + near_cols % clusters

    def apply_operator(panel_low):
        own_rows = lax.dynamic_slice_in_dim(panel_low, basis_owner * slab_rows, slab_rows, 1)
        partial_sum = jnp.einsum(
            "nrk,nrc->nkc", cluster_basis, own_rows, preferred_element_type=jnp.float32
        )
        projected = lax.psum(partial_sum, "basis").astype(jnp.bfloat16)
        projections_all = lax.all_gather(projected, "blk", axis=0, tiled=True)
        far_terms = jnp.einsum(
            "pkr,prc->pkc",
            coupling,
            projections_all[far_list[:, 1]],
            preferred_element_type=jnp.float32,
        )
        far_sum = jnp.einsum("np,pkc->nkc", far_table, far_terms, precision=highest_precision)
        far_low = far_sum.astype(jnp.bfloat16)
        pieces = []
        for offset in (1, -1):
            pieces.append(from_behind(panel_low, "blk", offset))
        window = jnp.concatenate([pieces[0], panel_low, pieces[1]], 0)
        source_vector = window[slot_index]
        near_field_products = jnp.einsum(
            "fpz,fzg->fpg", near_field_blocks, source_vector, preferred_element_type=jnp.float32
        )
        near_field_total = jnp.einsum(
            "id,dpb->ipb", row_lookup_table, near_field_products, precision=highest_precision
        )
        far_part = jnp.einsum(
            "nrk,nkc->nrc", cluster_basis, far_low, preferred_element_type=jnp.float32
        )
        return far_part + near_field_total

    krylov_one = apply_operator(right_panel.astype(jnp.bfloat16))
    second_low = lax.all_gather(krylov_one.astype(jnp.bfloat16), "basis", axis=1, tiled=True)
    krylov_two = apply_operator(second_low)
    return (krylov_one, krylov_two)


def on_device(right_panel, near_field_blocks, near_list, cluster_basis, coupling, far_list):
    cycle = lax.axis_size("blk")
    tiled = lax.axis_size("basis") == 2 and cluster_basis.shape[1] % 128 == 0 and cycle & (cycle - 1) == 0
    clusters = right_panel.shape[0]
    tiled = tiled and clusters & (clusters - 1) == 0
    run = tiled_on_device if tiled else general_on_device
    return run(right_panel, near_field_blocks, near_list, cluster_basis, coupling, far_list)


def solution(mesh):
    placed = (
        P(("groups", "blk"), None, "col"),
        P(("groups", "blk"), "basis", None),
        P(("groups", "blk"), None),
        P(("groups", "blk"), "basis", None),
        P(("groups", "blk"), None, None),
        P(("groups", "blk"), None),
    )
    return jax.shard_map(
        on_device,
        mesh=mesh,
        in_specs=placed,
        out_specs=(P(("groups", "blk"), "basis", "col"), P(("groups", "blk"), "basis", "col")),
        check_vma=False,
    )
```

```python
import functools

import jax
import jax.numpy as jnp
from jax import lax
from jax.experimental import pallas as pl
from jax.experimental.pallas import tpu as pltpu
from jax.sharding import PartitionSpec as P

UNROLL = 16
FIELD = 9
FAR_UNROLL = 32
VMEM = pl.BlockSpec(memory_space=pltpu.VMEM)
ANY = pl.BlockSpec(memory_space=pl.ANY)
HBM = pl.BlockSpec(memory_space=pltpu.HBM)
SMEM = pl.BlockSpec(memory_space=pltpu.SMEM)
TRANSPOSED_RHS = (((1,), (1,)), ((), ()))
PLAIN = (((1,), (0,)), ((), ()))


def swapped(array, axis, partner):
    return lax.ppermute(array, axis, [(i, partner(i)) for i in range(lax.axis_size(axis))])


def dot(a, b, dims):
    return lax.dot_general(a, b, dims, preferred_element_type=jnp.float32)


def params(mebibytes=14):
    return pltpu.CompilerParams(vmem_limit_bytes=mebibytes << 20)


def in_smem(array):
    return pltpu.with_memory_space_constraint(array, pltpu.SMEM)


def in_hbm(array):
    return pltpu.with_memory_space_constraint(array, pltpu.HBM)


def cost(microseconds):
    return pl.CostEstimate(flops=0, transcendentals=0, bytes_accessed=int(microseconds * 3.69e6))


def put_projection(low_ref, basis_ref, keep_ref, send_ref, at, parts):
    quarter = keep_ref.shape[0]
    for part in range(2):
        for n in range(quarter):
            m = 2 * part * quarter + n
            pair = [dot(low_ref[i], basis_ref[i], TRANSPOSED_RHS) for i in (m, m + quarter)]
            parts[part, n] = jnp.concatenate(pair, 1)
    keep_ref[...] = parts[lax.axis_index("basis")]
    send_ref[at:] = parts[1 - lax.axis_index("basis")].astype(jnp.bfloat16)


def start_kernel(panel_hbm, basis_hbm, mine_ref, basis_ref, keep_ref, send_ref, panel, parts, arrived):
    slab = basis_ref.shape[2]
    offset = pl.multiple_of(lax.axis_index("basis") * slab, slab)
    pieces = arrived.shape[0] // 2
    size = panel.shape[0] // pieces
    for i in range(pieces):
        rows = pl.ds(i * size, size)
        pltpu.make_async_copy(panel_hbm.at[rows, :, pl.ds(offset, slab)], panel.at[rows], arrived.at[i]).start()
        pltpu.make_async_copy(basis_hbm.at[rows], basis_ref.at[rows], arrived.at[pieces + i]).start()
    for i in range(pieces):
        rows = pl.ds(i * size, size)
        pltpu.make_async_copy(panel_hbm.at[rows, :, pl.ds(offset, slab)], panel.at[rows], arrived.at[i]).wait()
        mine_ref[rows] = panel[rows].astype(jnp.bfloat16)
    for i in range(pieces):
        rows = pl.ds(i * size, size)
        pltpu.make_async_copy(basis_hbm.at[rows], basis_ref.at[rows], arrived.at[pieces + i]).wait()
    put_projection(mine_ref, basis_ref, keep_ref, send_ref, 0, parts)


def put_sorted(words, kinds, nothing, plan_ref):
    count, width = words.shape[1], plan_ref.shape[1]
    across = jnp.broadcast_to(words, (count, count))
    down = across.T
    kind_across, kind_down = lax.shift_right_logical(across, 3 * FIELD), lax.shift_right_logical(down, 3 * FIELD)
    t = lax.broadcasted_iota(jnp.int32, (count, count), 1)
    s = lax.broadcasted_iota(jnp.int32, (count, count), 0)
    before = jnp.sum(((kind_across == kind_down) & (t < s)).astype(jnp.float32), 1, keepdims=True).astype(jnp.int32)
    word = down[:, :1]
    place = lax.broadcasted_iota(jnp.int32, (count, width), 1)
    slot = lax.broadcasted_iota(jnp.int32, (1, width), 1)
    totals = jnp.zeros((1, width), jnp.int32)
    for kind in range(kinds):
        of_kind = kind_down[:, :1] == kind
        total = jnp.sum(of_kind.astype(jnp.float32), 0, keepdims=True).astype(jnp.int32)
        row = jnp.sum(jnp.where(of_kind & (before == place), word, 0), 0, keepdims=True)
        plan_ref[kind : kind + 1] = jnp.where(slot < total, row, nothing)
        totals = jnp.where(slot == kind, total, totals)
    plan_ref[kinds : kinds + 1] = totals


def put_plans(clusters, near_ref, far_ref, near_plan, far_plan):
    here, basis = lax.axis_index("blk"), lax.axis_index("basis")
    bits, half = clusters.bit_length() - 1, clusters // 2
    rows, columns = near_ref[0:1], near_ref[1:2]
    entry = lax.broadcasted_iota(jnp.int32, rows.shape, 1)
    owner = lax.shift_right_logical(columns, bits)
    kind = jnp.where(owner == here, 0, jnp.where(owner == (here ^ 1), 2, 1))
    words = ((kind << FIELD | entry) << FIELD | (rows - here * clusters)) << FIELD | (columns & (clusters - 1))
    put_sorted(words, 3, clusters << FIELD, near_plan)
    rows, columns = far_ref[0:1], far_ref[1:2]
    entry = lax.broadcasted_iota(jnp.int32, rows.shape, 1)
    owner, source = lax.shift_right_logical(columns, bits), columns & (clusters - 1)
    kind = jnp.where(lax.shift_right_logical(source, bits - 1) == basis, 0, 1)
    place = (owner ^ here) * half + (source & (half - 1))
    words = ((kind << FIELD | entry) << FIELD | (rows - here * clusters)) << FIELD | place
    put_sorted(words, 2, clusters << FIELD, far_plan)


def prepare_kernel(clusters, near_hbm, far_hbm, blocks_hbm, coupling_hbm, *refs):
    near_plan_ref, far_plan_ref, blocks_ref, pairs_ref, coupling, turned, near_plan, far_plan, lists, arrived = refs

    def copies_of(source, target, pieces, first):
        size = target.shape[0] // pieces
        parts = [pl.ds(i * size, size) for i in range(pieces)]
        return [
            pltpu.make_async_copy(source.at[part], target.at[part], arrived.at[first + i])
            for i, part in enumerate(parts)
        ]

    coupling_copies = copies_of(coupling_hbm, coupling, 4, 0)
    block_copies = copies_of(blocks_hbm, blocks_ref, 8, 4)
    list_copies = [
        pltpu.make_async_copy(source, lists.at[i], arrived.at[14 + i]) for i, source in enumerate((near_hbm, far_hbm))
    ]
    for copy in list_copies + coupling_copies + block_copies:
        copy.start()
    for copy in list_copies:
        copy.wait()
    put_plans(clusters, lists.at[0], lists.at[1], near_plan, far_plan)
    plan_copies = [
        pltpu.make_async_copy(near_plan, near_plan_ref, arrived.at[12]),
        pltpu.make_async_copy(far_plan, far_plan_ref, arrived.at[13]),
    ]
    for copy in plan_copies:
        copy.start()
    rank, _, count = coupling.shape
    for copy in coupling_copies:
        copy.wait()
    for k in range(rank):
        turned[k * count : (k + 1) * count] = coupling[k].astype(jnp.float32).T
    for copy in plan_copies:
        copy.wait()

    def step(i, carry):
        for j in range(FAR_UNROLL):
            at = i * FAR_UNROLL + j
            pair = lax.shift_right_logical(far_plan_ref[0, at], 2 * FIELD) & ((1 << FIELD) - 1)
            pairs_ref[at] = turned[pl.ds(pair, rank, stride=count)].astype(jnp.bfloat16)
        return carry

    lax.fori_loop(0, lax.div(far_plan_ref[2, 0] + FAR_UNROLL - 1, FAR_UNROLL), step, 0)
    for copy in block_copies:
        copy.wait()


def add_near(plan_ref, kind, source_ref, blocks_ref, acc_ref):
    mask = (1 << FIELD) - 1

    def step(i, carry):
        words = [plan_ref[kind, i * UNROLL + j] for j in range(UNROLL)]
        terms = []
        for word in words:
            block = blocks_ref[lax.shift_right_logical(word, 2 * FIELD) & mask]
            terms.append(dot(source_ref[word & mask], block, TRANSPOSED_RHS))
        for word, term in zip(words, terms):
            row = lax.shift_right_logical(word, FIELD) & mask
            acc_ref[row] = acc_ref[row] + term
        return carry

    lax.fori_loop(0, lax.div(plan_ref[3, kind] + UNROLL - 1, UNROLL), step, 0)


def near_own_kernel(plan_ref, panel_hbm, blocks_ref, acc_ref, panel, low, arrived):
    copy = pltpu.make_async_copy(panel_hbm, panel, arrived)
    copy.start()
    acc_ref[...] = jnp.zeros_like(acc_ref)
    copy.wait()
    low[...] = panel[...].astype(jnp.bfloat16)
    add_near(plan_ref, 0, low, blocks_ref, acc_ref)


def put_whole(same_ref, other_ref, whole):
    slab = same_ref.shape[2]
    first = lax.axis_index("basis") == 0
    same, other = same_ref[...], other_ref[: same_ref.shape[0]]
    whole[:, :, :slab] = jnp.where(first, same, other)
    whole[:, :, slab:] = jnp.where(first, other, same)


def near_halves_kernel(kind, plan_ref, same_ref, other_ref, blocks_ref, *refs):
    acc_ref, whole = refs[-2:]
    put_whole(same_ref, other_ref, whole)
    acc_ref[...] = refs[0][...] if len(refs) == 3 else jnp.zeros_like(acc_ref)
    add_near(plan_ref, kind, whole, blocks_ref, acc_ref)


def far_kernel(plan_ref, pairs_ref, *refs):
    held, keep_ref, send_ref, unpacked, acc = refs[:-4], *refs[-4:]
    clusters = keep_ref.shape[0]
    quarter = held[0].shape[0]
    rank = pairs_ref.shape[1]
    mask = (1 << FIELD) - 1
    for d, packed in enumerate(held):
        unpacked[2 * d * quarter : (2 * d + 1) * quarter] = packed[:, :, :rank]
        unpacked[(2 * d + 1) * quarter : (2 * d + 2) * quarter] = packed[:, :, rank:]
    acc[...] = jnp.zeros_like(acc)

    def step(i, carry):
        words = [plan_ref[0, i * FAR_UNROLL + j] for j in range(FAR_UNROLL)]
        terms = []
        for j, word in enumerate(words):
            terms.append(dot(unpacked[word & mask], pairs_ref[i * FAR_UNROLL + j], TRANSPOSED_RHS))
        for word, term in zip(words, terms):
            row = lax.shift_right_logical(word, FIELD) & mask
            acc[row] = acc[row] + term
        return carry

    lax.fori_loop(0, lax.div(plan_ref[2, 0] + FAR_UNROLL - 1, FAR_UNROLL), step, 0)
    half = clusters // 2
    for n in range(half):
        keep_ref[n] = acc[n]
        keep_ref[n + half] = acc[n + half]
        send_ref[n] = jnp.concatenate([acc[n], acc[n + half]], 1).astype(jnp.bfloat16)


def finish_kernel(plan_ref, same_ref, other_ref, blocks_ref, acc_in, far_ref, far_other_ref, basis_ref, *refs):
    out_hbm, (acc_ref, whole, out_ref, sent) = refs[0], refs[-4:]
    near_halves_kernel(2, plan_ref, same_ref, other_ref, blocks_ref, acc_in, acc_ref, whole)
    half, _, wide = far_other_ref.shape
    rank = wide // 2
    pieces = sent.shape[0]
    size = 2 * half // pieces
    copies = []
    for n in range(2 * half):
        other = far_other_ref[n, :, :rank] if n < half else far_other_ref[n - half, :, rank:]
        far_low = (far_ref[n] + other.astype(jnp.float32)).astype(jnp.bfloat16)
        out_ref[n] = acc_ref[n] + dot(far_low, basis_ref[n], PLAIN)
        if (n + 1) % size == 0:
            rows = pl.ds(n + 1 - size, size)
            copies.append(pltpu.make_async_copy(out_ref.at[rows], out_hbm.at[rows], sent.at[n // size]))
            copies[-1].start()
    if len(refs) == 9:
        mine_ref, keep_ref, send_ref, parts = refs[1:5]
        low = out_ref[...].astype(jnp.bfloat16)
        mine_ref[...] = low
        send_ref[: 2 * half] = low
        put_projection(mine_ref, basis_ref, keep_ref, send_ref, 2 * half, parts)
    for copy in copies:
        copy.wait()


def tiled_on_device(right_panel, near_field_blocks, near_list, cluster_basis, coupling, far_list):
    clusters, points, columns = right_panel.shape
    near_count = near_list.shape[0]
    slab, rank = cluster_basis.shape[1:]
    panel = right_panel.transpose(0, 2, 1)
    basis = cluster_basis.transpose(0, 2, 1)
    cycle = lax.axis_size("blk")
    half, quarter = clusters // 2, clusters // 4
    f32, bf16 = jnp.float32, jnp.bfloat16
    mine_shape = jax.ShapeDtypeStruct((clusters, columns, slab), bf16)
    keep_shape = jax.ShapeDtypeStruct((quarter, columns, 2 * rank), f32)
    send_shape = jax.ShapeDtypeStruct((quarter, columns, 2 * rank), bf16)
    both_shape = jax.ShapeDtypeStruct((clusters + quarter, columns, slab), bf16)
    parts = pltpu.VMEM((2, quarter, columns, 2 * rank), f32)
    out_shape = jax.ShapeDtypeStruct((clusters, columns, slab), f32)
    acc_shape = jax.ShapeDtypeStruct((clusters + 1, columns, slab), f32)
    near_plan_shape = jax.ShapeDtypeStruct((4, near_count + UNROLL), jnp.int32)
    far_plan_shape = jax.ShapeDtypeStruct((3, far_list.shape[0] + FAR_UNROLL), jnp.int32)

    low_shape = jax.ShapeDtypeStruct((clusters, columns, points), bf16)
    pieces = 4
    mine, basis, keep, send = pl.pallas_call(
        start_kernel,
        out_shape=(mine_shape, jax.ShapeDtypeStruct(basis.shape, bf16), keep_shape, send_shape),
        in_specs=[HBM, HBM],
        out_specs=(VMEM,) * 4,
        scratch_shapes=[pltpu.VMEM(mine_shape.shape, f32), parts, pltpu.SemaphoreType.DMA((2 * pieces,))],
        compiler_params=params(),
        cost_estimate=cost(2),
        name="start",
    )(in_hbm(panel), in_hbm(basis))
    near_plan, far_plan, blocks, pairs = pl.pallas_call(
        functools.partial(prepare_kernel, clusters),
        out_shape=(
            pltpu.SMEM(near_plan_shape.shape, jnp.int32),
            pltpu.SMEM(far_plan_shape.shape, jnp.int32),
            pltpu.VMEM(near_field_blocks.shape, bf16),
            pltpu.VMEM((coupling.shape[0] + FAR_UNROLL, rank, rank), bf16),
        ),
        in_specs=[HBM] * 4,
        out_specs=(SMEM, SMEM, VMEM, VMEM),
        scratch_shapes=[
            pltpu.VMEM((rank, rank, coupling.shape[0]), bf16),
            pltpu.VMEM(((rank + 1) * coupling.shape[0], rank), f32),
            pltpu.VMEM(near_plan_shape.shape, jnp.int32),
            pltpu.VMEM(far_plan_shape.shape, jnp.int32),
            pltpu.VMEM((2, 2, near_count), jnp.int32),
            pltpu.SemaphoreType.DMA((16,)),
        ],
        compiler_params=params(20),
        cost_estimate=cost(4),
        name="prepare",
    )(*(in_hbm(array) for array in (near_list.T, far_list.T, near_field_blocks, coupling.transpose(1, 2, 0))))

    def near_own(plan, blocks):
        return pl.pallas_call(
            near_own_kernel,
            out_shape=acc_shape,
            in_specs=[SMEM, HBM, VMEM],
            out_specs=VMEM,
            scratch_shapes=[
                pltpu.VMEM(panel.shape, f32),
                pltpu.VMEM(low_shape.shape, bf16),
                pltpu.SemaphoreType.DMA,
            ],
            compiler_params=params(),
            cost_estimate=cost(3),
            name="near_own",
        )(in_smem(plan), panel, blocks)

    def near_halves(plan, blocks, kind, same, other, *acc):
        return pl.pallas_call(
            functools.partial(near_halves_kernel, kind),
            out_shape=acc_shape,
            in_specs=[SMEM] + [VMEM] * (3 + len(acc)),
            out_specs=VMEM,
            scratch_shapes=[pltpu.VMEM(low_shape.shape, bf16)],
            compiler_params=params(),
            cost_estimate=cost(2),
            name="near_halves",
        )(in_smem(plan), same, other, blocks, *acc)

    def far(plan, held):
        return pl.pallas_call(
            far_kernel,
            out_shape=(
                jax.ShapeDtypeStruct((clusters, columns, rank), f32),
                jax.ShapeDtypeStruct((half, columns, 2 * rank), bf16),
            ),
            in_specs=[SMEM, VMEM] + [VMEM] * len(held),
            out_specs=(VMEM, VMEM),
            scratch_shapes=[
                pltpu.VMEM((cycle * half, columns, rank), bf16),
                pltpu.VMEM((clusters + 1, columns, rank), f32),
            ],
            compiler_params=params(),
            cost_estimate=cost(3),
            name="far",
        )(in_smem(plan), pairs, *held)

    def finish(plan, blocks, same, other, acc, far_sum, far_other, last):
        outs = (out_shape,) if last else (out_shape, mine_shape, keep_shape, both_shape)
        return pl.pallas_call(
            finish_kernel,
            out_shape=outs,
            in_specs=[SMEM] + [VMEM] * 7,
            out_specs=(HBM,) + (VMEM,) * (len(outs) - 1),
            scratch_shapes=([] if last else [parts])
            + [pltpu.VMEM(acc_shape.shape, f32), pltpu.VMEM(low_shape.shape, bf16)]
            + [pltpu.VMEM(out_shape.shape, f32), pltpu.SemaphoreType.DMA((4,))],
            compiler_params=params(),
            cost_estimate=cost(4),
            name="finish",
        )(in_smem(plan), same, other, blocks, acc, far_sum, far_other, basis)

    def other_basis(array):
        return swapped(array, "basis", lambda i: 1 - i)

    def apply_operator(mine, keep, send, near_plan, last):
        crossing = swapped(mine, "blk", lambda i: (((i + 1) % cycle ^ 1) - 1) % cycle)
        paired = swapped(mine, "blk", lambda i: i ^ 1)
        received = other_basis(send)
        if last:
            acc = near_halves(near_plan, blocks, 0, mine, received)
        else:
            acc = near_own(near_plan, blocks)
        held = [(keep + received[-quarter:].astype(f32)).astype(bf16)]
        got = {0: held[0]}
        for d in reversed([1 << i for i in range(cycle.bit_length() - 1)]):
            for e in list(got):
                got[e ^ d] = swapped(got[e], "blk", lambda i, d=d: i ^ d)
        held = [got[d] for d in range(cycle)]
        if last:
            paired, acc, held[1], held[2] = lax.optimization_barrier((paired, acc, held[1], held[2]))
        else:
            paired, acc, held[2] = lax.optimization_barrier((paired, acc, held[2]))
        crossing_other = other_basis(crossing)
        paired_other = other_basis(paired)
        far_sum, far_send = far(far_plan, held)
        far_other = other_basis(far_send)
        acc = near_halves(near_plan, blocks, 1, crossing, crossing_other, acc)
        return finish(near_plan, blocks, paired, paired_other, acc, far_sum, far_other, last), near_plan

    (first, mine, keep, send), near_plan = apply_operator(mine, keep, send, near_plan, False)
    (second,), _ = apply_operator(mine, keep, send, near_plan, True)
    return first.transpose(0, 2, 1), second.transpose(0, 2, 1)


def from_behind(array, axis, by):
    size = lax.axis_size(axis)
    return lax.ppermute(array, axis, [(i, (i + by) % size) for i in range(size)])


def general_on_device(right_panel, near_field_blocks, near_list, cluster_basis, coupling, far_list):
    highest_precision = lax.Precision.HIGHEST
    clusters = right_panel.shape[0]
    slab_rows = cluster_basis.shape[1]
    cycle_place = lax.axis_index("blk")
    cycle_size = lax.axis_size("blk")
    basis_owner = lax.axis_index("basis")
    cluster_ids = jnp.arange(clusters, dtype=jnp.int32)
    near_rows = near_list[:, 0] - cycle_place * clusters
    near_cols = near_list[:, 1]
    row_lookup_table = (near_rows[None, :] == cluster_ids[:, None]).astype(jnp.float32)
    far_table = ((far_list[:, 0] - cycle_place * clusters)[None, :] == cluster_ids[:, None]).astype(
        jnp.float32
    )
    slot_index = (
        near_cols // clusters - cycle_place + 1 + cycle_size
    ) % cycle_size * clusters + near_cols % clusters

    def apply_operator(panel_low):
        own_rows = lax.dynamic_slice_in_dim(panel_low, basis_owner * slab_rows, slab_rows, 1)
        partial_sum = jnp.einsum(
            "nrk,nrc->nkc", cluster_basis, own_rows, preferred_element_type=jnp.float32
        )
        projected = lax.psum(partial_sum, "basis").astype(jnp.bfloat16)
        projections_all = lax.all_gather(projected, "blk", axis=0, tiled=True)
        far_terms = jnp.einsum(
            "pkr,prc->pkc",
            coupling,
            projections_all[far_list[:, 1]],
            preferred_element_type=jnp.float32,
        )
        far_sum = jnp.einsum("np,pkc->nkc", far_table, far_terms, precision=highest_precision)
        far_low = far_sum.astype(jnp.bfloat16)
        pieces = []
        for offset in (1, -1):
            pieces.append(from_behind(panel_low, "blk", offset))
        window = jnp.concatenate([pieces[0], panel_low, pieces[1]], 0)
        source_vector = window[slot_index]
        near_field_products = jnp.einsum(
            "fpz,fzg->fpg", near_field_blocks, source_vector, preferred_element_type=jnp.float32
        )
        near_field_total = jnp.einsum(
            "id,dpb->ipb", row_lookup_table, near_field_products, precision=highest_precision
        )
        far_part = jnp.einsum(
            "nrk,nkc->nrc", cluster_basis, far_low, preferred_element_type=jnp.float32
        )
        return far_part + near_field_total

    krylov_one = apply_operator(right_panel.astype(jnp.bfloat16))
    second_low = lax.all_gather(krylov_one.astype(jnp.bfloat16), "basis", axis=1, tiled=True)
    krylov_two = apply_operator(second_low)
    return (krylov_one, krylov_two)


def on_device(right_panel, near_field_blocks, near_list, cluster_basis, coupling, far_list):
    cycle = lax.axis_size("blk")
    tiled = lax.axis_size("basis") == 2 and cluster_basis.shape[1] % 128 == 0
    tiled = tiled and cycle >= 4 and cycle & (cycle - 1) == 0
    clusters = right_panel.shape[0]
    tiled = tiled and clusters & (clusters - 1) == 0
    run = tiled_on_device if tiled else general_on_device
    return run(right_panel, near_field_blocks, near_list, cluster_basis, coupling, far_list)


def solution(mesh):
    placed = (
        P(("groups", "blk"), None, "col"),
        P(("groups", "blk"), "basis", None),
        P(("groups", "blk"), None),
        P(("groups", "blk"), "basis", None),
        P(("groups", "blk"), None, None),
        P(("groups", "blk"), None),
    )
    return jax.shard_map(
        on_device,
        mesh=mesh,
        in_specs=placed,
        out_specs=(P(("groups", "blk"), "basis", "col"), P(("groups", "blk"), "basis", "col")),
        check_vma=False,
    )
```

```python
import functools

import jax
import jax.numpy as jnp
from jax import lax
from jax.experimental import pallas as pl
from jax.experimental.pallas import tpu as pltpu
from jax.sharding import PartitionSpec as P

UNROLL = 16
FIELD = 9
FAR_UNROLL = 16
VMEM = pl.BlockSpec(memory_space=pltpu.VMEM)
ANY = pl.BlockSpec(memory_space=pl.ANY)
HBM = pl.BlockSpec(memory_space=pltpu.HBM)
SMEM = pl.BlockSpec(memory_space=pltpu.SMEM)
TRANSPOSED_RHS = (((1,), (1,)), ((), ()))
PLAIN = (((1,), (0,)), ((), ()))


def swapped(array, axis, partner):
    return lax.ppermute(array, axis, [(i, partner(i)) for i in range(lax.axis_size(axis))])


def dot(a, b, dims):
    return lax.dot_general(a, b, dims, preferred_element_type=jnp.float32)


def params(mebibytes=14):
    return pltpu.CompilerParams(vmem_limit_bytes=mebibytes << 20)


def in_smem(array):
    return pltpu.with_memory_space_constraint(array, pltpu.SMEM)


def in_hbm(array):
    return pltpu.with_memory_space_constraint(array, pltpu.HBM)


def cost(microseconds):
    return pl.CostEstimate(flops=0, transcendentals=0, bytes_accessed=int(microseconds * 3.69e6))


def put_projection(low_ref, basis_ref, keep_ref, send_ref, at, parts):
    quarter = keep_ref.shape[0]
    for part in range(2):
        for n in range(quarter):
            m = 2 * part * quarter + n
            pair = [dot(low_ref[i], basis_ref[i], TRANSPOSED_RHS) for i in (m, m + quarter)]
            parts[part, n] = jnp.concatenate(pair, 1)
    keep_ref[...] = parts[lax.axis_index("basis")]
    send_ref[at:] = parts[1 - lax.axis_index("basis")].astype(jnp.bfloat16)


def start_kernel(panel_hbm, basis_hbm, mine_ref, basis_ref, keep_ref, send_ref, panel, parts, arrived):
    slab = basis_ref.shape[2]
    offset = pl.multiple_of(lax.axis_index("basis") * slab, slab)
    pieces = arrived.shape[0] // 2
    size = panel.shape[0] // pieces
    for i in range(pieces):
        rows = pl.ds(i * size, size)
        pltpu.make_async_copy(panel_hbm.at[rows, :, pl.ds(offset, slab)], panel.at[rows], arrived.at[i]).start()
        pltpu.make_async_copy(basis_hbm.at[rows], basis_ref.at[rows], arrived.at[pieces + i]).start()
    for i in range(pieces):
        rows = pl.ds(i * size, size)
        pltpu.make_async_copy(panel_hbm.at[rows, :, pl.ds(offset, slab)], panel.at[rows], arrived.at[i]).wait()
        mine_ref[rows] = panel[rows].astype(jnp.bfloat16)
    for i in range(pieces):
        rows = pl.ds(i * size, size)
        pltpu.make_async_copy(basis_hbm.at[rows], basis_ref.at[rows], arrived.at[pieces + i]).wait()
    put_projection(mine_ref, basis_ref, keep_ref, send_ref, 0, parts)


def put_sorted(words, kinds, nothing, plan_ref):
    count, width = words.shape[1], plan_ref.shape[1]
    across = jnp.broadcast_to(words, (count, count))
    down = across.T
    kind_across, kind_down = lax.shift_right_logical(across, 3 * FIELD), lax.shift_right_logical(down, 3 * FIELD)
    t = lax.broadcasted_iota(jnp.int32, (count, count), 1)
    s = lax.broadcasted_iota(jnp.int32, (count, count), 0)
    before = jnp.sum(((kind_across == kind_down) & (t < s)).astype(jnp.float32), 1, keepdims=True).astype(jnp.int32)
    word = down[:, :1]
    place = lax.broadcasted_iota(jnp.int32, (count, width), 1)
    slot = lax.broadcasted_iota(jnp.int32, (1, width), 1)
    totals = jnp.zeros((1, width), jnp.int32)
    for kind in range(kinds):
        of_kind = kind_down[:, :1] == kind
        total = jnp.sum(of_kind.astype(jnp.float32), 0, keepdims=True).astype(jnp.int32)
        row = jnp.sum(jnp.where(of_kind & (before == place), word, 0), 0, keepdims=True)
        plan_ref[kind : kind + 1] = jnp.where(slot < total, row, nothing)
        totals = jnp.where(slot == kind, total, totals)
    plan_ref[kinds : kinds + 1] = totals


def put_plans(clusters, near_ref, far_ref, near_plan, far_plan):
    here, basis = lax.axis_index("blk"), lax.axis_index("basis")
    bits, half = clusters.bit_length() - 1, clusters // 2
    rows, columns = near_ref[0:1], near_ref[1:2]
    entry = lax.broadcasted_iota(jnp.int32, rows.shape, 1)
    owner = lax.shift_right_logical(columns, bits)
    kind = jnp.where(owner == here, 0, jnp.where(owner == (here ^ 1), 2, 1))
    words = ((kind << FIELD | entry) << FIELD | (rows - here * clusters)) << FIELD | (columns & (clusters - 1))
    put_sorted(words, 3, clusters << FIELD, near_plan)
    rows, columns = far_ref[0:1], far_ref[1:2]
    entry = lax.broadcasted_iota(jnp.int32, rows.shape, 1)
    owner, source = lax.shift_right_logical(columns, bits), columns & (clusters - 1)
    kind = jnp.where(lax.shift_right_logical(source, bits - 1) == basis, 0, 1)
    place = (owner ^ here) * half + (source & (half - 1))
    words = ((kind << FIELD | entry) << FIELD | (rows - here * clusters)) << FIELD | place
    put_sorted(words, 2, clusters << FIELD, far_plan)


def prepare_kernel(clusters, near_hbm, far_hbm, blocks_hbm, coupling_hbm, *refs):
    near_plan_ref, far_plan_ref, blocks_ref, pairs_ref, coupling, turned, near_plan, far_plan, lists, arrived = refs

    def copies_of(source, target, pieces, first):
        size = target.shape[0] // pieces
        parts = [pl.ds(i * size, size) for i in range(pieces)]
        return [
            pltpu.make_async_copy(source.at[part], target.at[part], arrived.at[first + i])
            for i, part in enumerate(parts)
        ]

    coupling_copies = copies_of(coupling_hbm, coupling, 4, 0)
    block_copies = copies_of(blocks_hbm, blocks_ref, 8, 4)
    list_copies = [
        pltpu.make_async_copy(source, lists.at[i], arrived.at[14 + i]) for i, source in enumerate((near_hbm, far_hbm))
    ]
    for copy in list_copies + coupling_copies + block_copies:
        copy.start()
    for copy in list_copies:
        copy.wait()
    put_plans(clusters, lists.at[0], lists.at[1], near_plan, far_plan)
    plan_copies = [
        pltpu.make_async_copy(near_plan, near_plan_ref, arrived.at[12]),
        pltpu.make_async_copy(far_plan, far_plan_ref, arrived.at[13]),
    ]
    for copy in plan_copies:
        copy.start()
    rank, _, count = coupling.shape
    for copy in coupling_copies:
        copy.wait()
    for k in range(rank):
        turned[k * count : (k + 1) * count] = coupling[k].astype(jnp.float32).T
    for copy in plan_copies:
        copy.wait()

    def step(i, carry):
        for j in range(FAR_UNROLL):
            at = i * FAR_UNROLL + j
            pair = lax.shift_right_logical(far_plan_ref[0, at], 2 * FIELD) & ((1 << FIELD) - 1)
            pairs_ref[at] = turned[pl.ds(pair, rank, stride=count)].astype(jnp.bfloat16)
        return carry

    lax.fori_loop(0, lax.div(far_plan_ref[2, 0] + FAR_UNROLL - 1, FAR_UNROLL), step, 0)
    for copy in block_copies:
        copy.wait()


def add_near(plan_ref, kind, source_ref, blocks_ref, acc_ref):
    mask = (1 << FIELD) - 1

    def step(i, carry):
        words = [plan_ref[kind, i * UNROLL + j] for j in range(UNROLL)]
        terms = []
        for word in words:
            block = blocks_ref[lax.shift_right_logical(word, 2 * FIELD) & mask]
            terms.append(dot(source_ref[word & mask], block, TRANSPOSED_RHS))
        for word, term in zip(words, terms):
            row = lax.shift_right_logical(word, FIELD) & mask
            acc_ref[row] = acc_ref[row] + term
        return carry

    lax.fori_loop(0, lax.div(plan_ref[3, kind] + UNROLL - 1, UNROLL), step, 0)


def near_own_kernel(plan_ref, panel_hbm, blocks_ref, acc_ref, panel, low, arrived):
    copy = pltpu.make_async_copy(panel_hbm, panel, arrived)
    copy.start()
    acc_ref[...] = jnp.zeros_like(acc_ref)
    copy.wait()
    low[...] = panel[...].astype(jnp.bfloat16)
    add_near(plan_ref, 0, low, blocks_ref, acc_ref)


def put_whole(same_ref, other_ref, whole):
    slab = same_ref.shape[2]
    first = lax.axis_index("basis") == 0
    same, other = same_ref[...], other_ref[: same_ref.shape[0]]
    whole[:, :, :slab] = jnp.where(first, same, other)
    whole[:, :, slab:] = jnp.where(first, other, same)


def near_halves_kernel(kind, plan_ref, same_ref, other_ref, blocks_ref, *refs):
    acc_ref, whole = refs[-2:]
    put_whole(same_ref, other_ref, whole)
    acc_ref[...] = refs[0][...] if len(refs) == 3 else jnp.zeros_like(acc_ref)
    add_near(plan_ref, kind, whole, blocks_ref, acc_ref)


def far_kernel(plan_ref, pairs_ref, *refs):
    held, keep_ref, send_ref, unpacked, acc = refs[:-4], *refs[-4:]
    clusters = keep_ref.shape[0]
    quarter = held[0].shape[0]
    rank = pairs_ref.shape[1]
    mask = (1 << FIELD) - 1
    for d, packed in enumerate(held):
        unpacked[2 * d * quarter : (2 * d + 1) * quarter] = packed[:, :, :rank]
        unpacked[(2 * d + 1) * quarter : (2 * d + 2) * quarter] = packed[:, :, rank:]
    acc[...] = jnp.zeros_like(acc)

    def step(i, carry):
        words = [plan_ref[0, i * FAR_UNROLL + j] for j in range(FAR_UNROLL)]
        terms = []
        for j, word in enumerate(words):
            terms.append(dot(unpacked[word & mask], pairs_ref[i * FAR_UNROLL + j], TRANSPOSED_RHS))
        for word, term in zip(words, terms):
            row = lax.shift_right_logical(word, FIELD) & mask
            acc[row] = acc[row] + term
        return carry

    lax.fori_loop(0, lax.div(plan_ref[2, 0] + FAR_UNROLL - 1, FAR_UNROLL), step, 0)
    half = clusters // 2
    for n in range(half):
        keep_ref[n] = acc[n]
        keep_ref[n + half] = acc[n + half]
        send_ref[n] = jnp.concatenate([acc[n], acc[n + half]], 1).astype(jnp.bfloat16)


def finish_kernel(plan_ref, same_ref, other_ref, blocks_ref, acc_in, far_ref, far_other_ref, basis_ref, *refs):
    out_hbm, (acc_ref, whole, out_ref, sent) = refs[0], refs[-4:]
    near_halves_kernel(2, plan_ref, same_ref, other_ref, blocks_ref, acc_in, acc_ref, whole)
    half, _, wide = far_other_ref.shape
    rank = wide // 2
    pieces = sent.shape[0]
    size = 2 * half // pieces
    copies = []
    for n in range(2 * half):
        other = far_other_ref[n, :, :rank] if n < half else far_other_ref[n - half, :, rank:]
        far_low = (far_ref[n] + other.astype(jnp.float32)).astype(jnp.bfloat16)
        out_ref[n] = acc_ref[n] + dot(far_low, basis_ref[n], PLAIN)
        if (n + 1) % size == 0:
            rows = pl.ds(n + 1 - size, size)
            copies.append(pltpu.make_async_copy(out_ref.at[rows], out_hbm.at[rows], sent.at[n // size]))
            copies[-1].start()
    if len(refs) == 9:
        mine_ref, keep_ref, send_ref, parts = refs[1:5]
        low = out_ref[...].astype(jnp.bfloat16)
        mine_ref[...] = low
        send_ref[: 2 * half] = low
        put_projection(mine_ref, basis_ref, keep_ref, send_ref, 2 * half, parts)
    for copy in copies:
        copy.wait()


def tiled_on_device(right_panel, near_field_blocks, near_list, cluster_basis, coupling, far_list):
    clusters, points, columns = right_panel.shape
    near_count = near_list.shape[0]
    slab, rank = cluster_basis.shape[1:]
    panel = right_panel.transpose(0, 2, 1)
    basis = cluster_basis.transpose(0, 2, 1)
    cycle = lax.axis_size("blk")
    half, quarter = clusters // 2, clusters // 4
    f32, bf16 = jnp.float32, jnp.bfloat16
    mine_shape = jax.ShapeDtypeStruct((clusters, columns, slab), bf16)
    keep_shape = jax.ShapeDtypeStruct((quarter, columns, 2 * rank), f32)
    send_shape = jax.ShapeDtypeStruct((quarter, columns, 2 * rank), bf16)
    both_shape = jax.ShapeDtypeStruct((clusters + quarter, columns, slab), bf16)
    parts = pltpu.VMEM((2, quarter, columns, 2 * rank), f32)
    out_shape = jax.ShapeDtypeStruct((clusters, columns, slab), f32)
    acc_shape = jax.ShapeDtypeStruct((clusters + 1, columns, slab), f32)
    near_plan_shape = jax.ShapeDtypeStruct((4, near_count + UNROLL), jnp.int32)
    far_plan_shape = jax.ShapeDtypeStruct((3, far_list.shape[0] + FAR_UNROLL), jnp.int32)

    low_shape = jax.ShapeDtypeStruct((clusters, columns, points), bf16)
    pieces = 4
    mine, basis, keep, send = pl.pallas_call(
        start_kernel,
        out_shape=(mine_shape, jax.ShapeDtypeStruct(basis.shape, bf16), keep_shape, send_shape),
        in_specs=[HBM, HBM],
        out_specs=(VMEM,) * 4,
        scratch_shapes=[pltpu.VMEM(mine_shape.shape, f32), parts, pltpu.SemaphoreType.DMA((2 * pieces,))],
        compiler_params=params(),
        cost_estimate=cost(2),
        name="start",
    )(in_hbm(panel), in_hbm(basis))
    near_plan, far_plan, blocks, pairs = pl.pallas_call(
        functools.partial(prepare_kernel, clusters),
        out_shape=(
            pltpu.SMEM(near_plan_shape.shape, jnp.int32),
            pltpu.SMEM(far_plan_shape.shape, jnp.int32),
            pltpu.VMEM(near_field_blocks.shape, bf16),
            pltpu.VMEM((coupling.shape[0] + FAR_UNROLL, rank, rank), bf16),
        ),
        in_specs=[HBM] * 4,
        out_specs=(SMEM, SMEM, VMEM, VMEM),
        scratch_shapes=[
            pltpu.VMEM((rank, rank, coupling.shape[0]), bf16),
            pltpu.VMEM(((rank + 1) * coupling.shape[0], rank), f32),
            pltpu.VMEM(near_plan_shape.shape, jnp.int32),
            pltpu.VMEM(far_plan_shape.shape, jnp.int32),
            pltpu.VMEM((2, 2, near_count), jnp.int32),
            pltpu.SemaphoreType.DMA((16,)),
        ],
        compiler_params=params(20),
        cost_estimate=cost(4),
        name="prepare",
    )(*(in_hbm(array) for array in (near_list.T, far_list.T, near_field_blocks, coupling.transpose(1, 2, 0))))

    def near_own(plan, blocks):
        return pl.pallas_call(
            near_own_kernel,
            out_shape=acc_shape,
            in_specs=[SMEM, HBM, VMEM],
            out_specs=VMEM,
            scratch_shapes=[
                pltpu.VMEM(panel.shape, f32),
                pltpu.VMEM(low_shape.shape, bf16),
                pltpu.SemaphoreType.DMA,
            ],
            compiler_params=params(),
            cost_estimate=cost(3),
            name="near_own",
        )(in_smem(plan), panel, blocks)

    def near_halves(plan, blocks, kind, same, other, *acc):
        return pl.pallas_call(
            functools.partial(near_halves_kernel, kind),
            out_shape=acc_shape,
            in_specs=[SMEM] + [VMEM] * (3 + len(acc)),
            out_specs=VMEM,
            scratch_shapes=[pltpu.VMEM(low_shape.shape, bf16)],
            compiler_params=params(),
            cost_estimate=cost(2),
            name="near_halves",
        )(in_smem(plan), same, other, blocks, *acc)

    def far(plan, held):
        return pl.pallas_call(
            far_kernel,
            out_shape=(
                jax.ShapeDtypeStruct((clusters, columns, rank), f32),
                jax.ShapeDtypeStruct((half, columns, 2 * rank), bf16),
            ),
            in_specs=[SMEM, VMEM] + [VMEM] * len(held),
            out_specs=(VMEM, VMEM),
            scratch_shapes=[
                pltpu.VMEM((cycle * half, columns, rank), bf16),
                pltpu.VMEM((clusters + 1, columns, rank), f32),
            ],
            compiler_params=params(),
            cost_estimate=cost(3),
            name="far",
        )(in_smem(plan), pairs, *held)

    def finish(plan, blocks, same, other, acc, far_sum, far_other, last):
        outs = (out_shape,) if last else (out_shape, mine_shape, keep_shape, both_shape)
        return pl.pallas_call(
            finish_kernel,
            out_shape=outs,
            in_specs=[SMEM] + [VMEM] * 7,
            out_specs=(HBM,) + (VMEM,) * (len(outs) - 1),
            scratch_shapes=([] if last else [parts])
            + [pltpu.VMEM(acc_shape.shape, f32), pltpu.VMEM(low_shape.shape, bf16)]
            + [pltpu.VMEM(out_shape.shape, f32), pltpu.SemaphoreType.DMA((4,))],
            compiler_params=params(),
            cost_estimate=cost(4),
            name="finish",
        )(in_smem(plan), same, other, blocks, acc, far_sum, far_other, basis)

    def other_basis(array):
        return swapped(array, "basis", lambda i: 1 - i)

    def apply_operator(mine, keep, send, near_plan, last):
        crossing = swapped(mine, "blk", lambda i: (((i + 1) % cycle ^ 1) - 1) % cycle)
        paired = swapped(mine, "blk", lambda i: i ^ 1)
        received = other_basis(send)
        if last:
            acc = near_halves(near_plan, blocks, 0, mine, received)
        else:
            acc = near_own(near_plan, blocks)
        held = [(keep + received[-quarter:].astype(f32)).astype(bf16)]
        got = {0: held[0]}
        for d in reversed([1 << i for i in range(cycle.bit_length() - 1)]):
            for e in list(got):
                got[e ^ d] = swapped(got[e], "blk", lambda i, d=d: i ^ d)
        held = [got[d] for d in range(cycle)]
        if last:
            paired, acc, held[1], held[2] = lax.optimization_barrier((paired, acc, held[1], held[2]))
        else:
            paired, acc, held[2] = lax.optimization_barrier((paired, acc, held[2]))
        crossing_other = other_basis(crossing)
        paired_other = other_basis(paired)
        far_sum, far_send = far(far_plan, held)
        far_other = other_basis(far_send)
        acc = near_halves(near_plan, blocks, 1, crossing, crossing_other, acc)
        return finish(near_plan, blocks, paired, paired_other, acc, far_sum, far_other, last), near_plan

    (first, mine, keep, send), near_plan = apply_operator(mine, keep, send, near_plan, False)
    (second,), _ = apply_operator(mine, keep, send, near_plan, True)
    return first.transpose(0, 2, 1), second.transpose(0, 2, 1)


def from_behind(array, axis, by):
    size = lax.axis_size(axis)
    return lax.ppermute(array, axis, [(i, (i + by) % size) for i in range(size)])


def general_on_device(right_panel, near_field_blocks, near_list, cluster_basis, coupling, far_list):
    highest_precision = lax.Precision.HIGHEST
    clusters = right_panel.shape[0]
    slab_rows = cluster_basis.shape[1]
    cycle_place = lax.axis_index("blk")
    cycle_size = lax.axis_size("blk")
    basis_owner = lax.axis_index("basis")
    cluster_ids = jnp.arange(clusters, dtype=jnp.int32)
    near_rows = near_list[:, 0] - cycle_place * clusters
    near_cols = near_list[:, 1]
    row_lookup_table = (near_rows[None, :] == cluster_ids[:, None]).astype(jnp.float32)
    far_table = ((far_list[:, 0] - cycle_place * clusters)[None, :] == cluster_ids[:, None]).astype(
        jnp.float32
    )
    slot_index = (
        near_cols // clusters - cycle_place + 1 + cycle_size
    ) % cycle_size * clusters + near_cols % clusters

    def apply_operator(panel_low):
        own_rows = lax.dynamic_slice_in_dim(panel_low, basis_owner * slab_rows, slab_rows, 1)
        partial_sum = jnp.einsum(
            "nrk,nrc->nkc", cluster_basis, own_rows, preferred_element_type=jnp.float32
        )
        projected = lax.psum(partial_sum, "basis").astype(jnp.bfloat16)
        projections_all = lax.all_gather(projected, "blk", axis=0, tiled=True)
        far_terms = jnp.einsum(
            "pkr,prc->pkc",
            coupling,
            projections_all[far_list[:, 1]],
            preferred_element_type=jnp.float32,
        )
        far_sum = jnp.einsum("np,pkc->nkc", far_table, far_terms, precision=highest_precision)
        far_low = far_sum.astype(jnp.bfloat16)
        pieces = []
        for offset in (1, -1):
            pieces.append(from_behind(panel_low, "blk", offset))
        window = jnp.concatenate([pieces[0], panel_low, pieces[1]], 0)
        source_vector = window[slot_index]
        near_field_products = jnp.einsum(
            "fpz,fzg->fpg", near_field_blocks, source_vector, preferred_element_type=jnp.float32
        )
        near_field_total = jnp.einsum(
            "id,dpb->ipb", row_lookup_table, near_field_products, precision=highest_precision
        )
        far_part = jnp.einsum(
            "nrk,nkc->nrc", cluster_basis, far_low, preferred_element_type=jnp.float32
        )
        return far_part + near_field_total

    krylov_one = apply_operator(right_panel.astype(jnp.bfloat16))
    second_low = lax.all_gather(krylov_one.astype(jnp.bfloat16), "basis", axis=1, tiled=True)
    krylov_two = apply_operator(second_low)
    return (krylov_one, krylov_two)


def on_device(right_panel, near_field_blocks, near_list, cluster_basis, coupling, far_list):
    cycle = lax.axis_size("blk")
    tiled = lax.axis_size("basis") == 2 and cluster_basis.shape[1] % 128 == 0
    tiled = tiled and cycle >= 4 and cycle & (cycle - 1) == 0
    clusters = right_panel.shape[0]
    tiled = tiled and clusters & (clusters - 1) == 0
    run = tiled_on_device if tiled else general_on_device
    return run(right_panel, near_field_blocks, near_list, cluster_basis, coupling, far_list)


def solution(mesh):
    placed = (
        P(("groups", "blk"), None, "col"),
        P(("groups", "blk"), "basis", None),
        P(("groups", "blk"), None),
        P(("groups", "blk"), "basis", None),
        P(("groups", "blk"), None, None),
        P(("groups", "blk"), None),
    )
    return jax.shard_map(
        on_device,
        mesh=mesh,
        in_specs=placed,
        out_specs=(P(("groups", "blk"), "basis", "col"), P(("groups", "blk"), "basis", "col")),
        check_vma=False,
    )
```

```python
import functools

import jax
import jax.numpy as jnp
from jax import lax
from jax.experimental import pallas as pl
from jax.experimental.pallas import tpu as pltpu
from jax.sharding import PartitionSpec as P

UNROLL = 24
FIELD = 9
FAR_UNROLL = 32
VMEM = pl.BlockSpec(memory_space=pltpu.VMEM)
ANY = pl.BlockSpec(memory_space=pl.ANY)
HBM = pl.BlockSpec(memory_space=pltpu.HBM)
SMEM = pl.BlockSpec(memory_space=pltpu.SMEM)
TRANSPOSED_RHS = (((1,), (1,)), ((), ()))
PLAIN = (((1,), (0,)), ((), ()))


def swapped(array, axis, partner):
    return lax.ppermute(array, axis, [(i, partner(i)) for i in range(lax.axis_size(axis))])


def dot(a, b, dims):
    return lax.dot_general(a, b, dims, preferred_element_type=jnp.float32)


def params(mebibytes=14):
    return pltpu.CompilerParams(vmem_limit_bytes=mebibytes << 20)


def in_smem(array):
    return pltpu.with_memory_space_constraint(array, pltpu.SMEM)


def in_hbm(array):
    return pltpu.with_memory_space_constraint(array, pltpu.HBM)


def cost(microseconds):
    return pl.CostEstimate(flops=0, transcendentals=0, bytes_accessed=int(microseconds * 3.69e6))


def put_projection(low_ref, basis_ref, keep_ref, send_ref, at, parts):
    quarter = keep_ref.shape[0]
    for part in range(2):
        for n in range(quarter):
            m = 2 * part * quarter + n
            pair = [dot(low_ref[i], basis_ref[i], TRANSPOSED_RHS) for i in (m, m + quarter)]
            parts[part, n] = jnp.concatenate(pair, 1)
    keep_ref[...] = parts[lax.axis_index("basis")]
    send_ref[at:] = parts[1 - lax.axis_index("basis")].astype(jnp.bfloat16)


def start_kernel(panel_hbm, basis_hbm, mine_ref, basis_ref, keep_ref, send_ref, panel, parts, arrived):
    slab = basis_ref.shape[2]
    offset = pl.multiple_of(lax.axis_index("basis") * slab, slab)
    pieces = arrived.shape[0] // 2
    size = panel.shape[0] // pieces
    for i in range(pieces):
        rows = pl.ds(i * size, size)
        pltpu.make_async_copy(panel_hbm.at[rows, :, pl.ds(offset, slab)], panel.at[rows], arrived.at[i]).start()
        pltpu.make_async_copy(basis_hbm.at[rows], basis_ref.at[rows], arrived.at[pieces + i]).start()
    for i in range(pieces):
        rows = pl.ds(i * size, size)
        pltpu.make_async_copy(panel_hbm.at[rows, :, pl.ds(offset, slab)], panel.at[rows], arrived.at[i]).wait()
        mine_ref[rows] = panel[rows].astype(jnp.bfloat16)
    for i in range(pieces):
        rows = pl.ds(i * size, size)
        pltpu.make_async_copy(basis_hbm.at[rows], basis_ref.at[rows], arrived.at[pieces + i]).wait()
    put_projection(mine_ref, basis_ref, keep_ref, send_ref, 0, parts)


def put_sorted(words, kinds, nothing, plan_ref):
    count, width = words.shape[1], plan_ref.shape[1]
    across = jnp.broadcast_to(words, (count, count))
    down = across.T
    kind_across, kind_down = lax.shift_right_logical(across, 3 * FIELD), lax.shift_right_logical(down, 3 * FIELD)
    t = lax.broadcasted_iota(jnp.int32, (count, count), 1)
    s = lax.broadcasted_iota(jnp.int32, (count, count), 0)
    before = jnp.sum(((kind_across == kind_down) & (t < s)).astype(jnp.float32), 1, keepdims=True).astype(jnp.int32)
    word = down[:, :1]
    place = lax.broadcasted_iota(jnp.int32, (count, width), 1)
    slot = lax.broadcasted_iota(jnp.int32, (1, width), 1)
    totals = jnp.zeros((1, width), jnp.int32)
    for kind in range(kinds):
        of_kind = kind_down[:, :1] == kind
        total = jnp.sum(of_kind.astype(jnp.float32), 0, keepdims=True).astype(jnp.int32)
        row = jnp.sum(jnp.where(of_kind & (before == place), word, 0), 0, keepdims=True)
        plan_ref[kind : kind + 1] = jnp.where(slot < total, row, nothing)
        totals = jnp.where(slot == kind, total, totals)
    plan_ref[kinds : kinds + 1] = totals


def put_plans(clusters, near_ref, far_ref, near_plan, far_plan):
    here, basis = lax.axis_index("blk"), lax.axis_index("basis")
    bits, half = clusters.bit_length() - 1, clusters // 2
    rows, columns = near_ref[0:1], near_ref[1:2]
    entry = lax.broadcasted_iota(jnp.int32, rows.shape, 1)
    owner = lax.shift_right_logical(columns, bits)
    kind = jnp.where(owner == here, 0, jnp.where(owner == (here ^ 1), 2, 1))
    words = ((kind << FIELD | entry) << FIELD | (rows - here * clusters)) << FIELD | (columns & (clusters - 1))
    put_sorted(words, 3, clusters << FIELD, near_plan)
    rows, columns = far_ref[0:1], far_ref[1:2]
    entry = lax.broadcasted_iota(jnp.int32, rows.shape, 1)
    owner, source = lax.shift_right_logical(columns, bits), columns & (clusters - 1)
    kind = jnp.where(lax.shift_right_logical(source, bits - 1) == basis, 0, 1)
    place = (owner ^ here) * half + (source & (half - 1))
    words = ((kind << FIELD | entry) << FIELD | (rows - here * clusters)) << FIELD | place
    put_sorted(words, 2, clusters << FIELD, far_plan)


def prepare_kernel(clusters, near_hbm, far_hbm, blocks_hbm, coupling_hbm, *refs):
    near_plan_ref, far_plan_ref, blocks_ref, pairs_ref, coupling, turned, near_plan, far_plan, lists, arrived = refs

    def copies_of(source, target, pieces, first):
        size = target.shape[0] // pieces
        parts = [pl.ds(i * size, size) for i in range(pieces)]
        return [
            pltpu.make_async_copy(source.at[part], target.at[part], arrived.at[first + i])
            for i, part in enumerate(parts)
        ]

    coupling_copies = copies_of(coupling_hbm, coupling, 4, 0)
    block_copies = copies_of(blocks_hbm, blocks_ref, 8, 4)
    list_copies = [
        pltpu.make_async_copy(source, lists.at[i], arrived.at[14 + i]) for i, source in enumerate((near_hbm, far_hbm))
    ]
    for copy in list_copies + coupling_copies + block_copies:
        copy.start()
    for copy in list_copies:
        copy.wait()
    put_plans(clusters, lists.at[0], lists.at[1], near_plan, far_plan)
    plan_copies = [
        pltpu.make_async_copy(near_plan, near_plan_ref, arrived.at[12]),
        pltpu.make_async_copy(far_plan, far_plan_ref, arrived.at[13]),
    ]
    for copy in plan_copies:
        copy.start()
    rank, _, count = coupling.shape
    for copy in coupling_copies:
        copy.wait()
    for k in range(rank):
        turned[k * count : (k + 1) * count] = coupling[k].astype(jnp.float32).T
    for copy in plan_copies:
        copy.wait()

    def step(i, carry):
        for j in range(FAR_UNROLL):
            at = i * FAR_UNROLL + j
            pair = lax.shift_right_logical(far_plan_ref[0, at], 2 * FIELD) & ((1 << FIELD) - 1)
            pairs_ref[at] = turned[pl.ds(pair, rank, stride=count)].astype(jnp.bfloat16)
        return carry

    lax.fori_loop(0, lax.div(far_plan_ref[2, 0] + FAR_UNROLL - 1, FAR_UNROLL), step, 0)
    for copy in block_copies:
        copy.wait()


def add_near(plan_ref, kind, source_ref, blocks_ref, acc_ref):
    mask = (1 << FIELD) - 1

    def step(i, carry):
        words = [plan_ref[kind, i * UNROLL + j] for j in range(UNROLL)]
        terms = []
        for word in words:
            block = blocks_ref[lax.shift_right_logical(word, 2 * FIELD) & mask]
            terms.append(dot(source_ref[word & mask], block, TRANSPOSED_RHS))
        for word, term in zip(words, terms):
            row = lax.shift_right_logical(word, FIELD) & mask
            acc_ref[row] = acc_ref[row] + term
        return carry

    lax.fori_loop(0, lax.div(plan_ref[3, kind] + UNROLL - 1, UNROLL), step, 0)


def near_own_kernel(plan_ref, panel_hbm, blocks_ref, acc_ref, panel, low, arrived):
    copy = pltpu.make_async_copy(panel_hbm, panel, arrived)
    copy.start()
    acc_ref[...] = jnp.zeros_like(acc_ref)
    copy.wait()
    low[...] = panel[...].astype(jnp.bfloat16)
    add_near(plan_ref, 0, low, blocks_ref, acc_ref)


def put_whole(same_ref, other_ref, whole):
    slab = same_ref.shape[2]
    first = lax.axis_index("basis") == 0
    same, other = same_ref[...], other_ref[: same_ref.shape[0]]
    whole[:, :, :slab] = jnp.where(first, same, other)
    whole[:, :, slab:] = jnp.where(first, other, same)


def near_halves_kernel(kind, plan_ref, same_ref, other_ref, blocks_ref, *refs):
    acc_ref, whole = refs[-2:]
    put_whole(same_ref, other_ref, whole)
    acc_ref[...] = refs[0][...] if len(refs) == 3 else jnp.zeros_like(acc_ref)
    add_near(plan_ref, kind, whole, blocks_ref, acc_ref)


def far_kernel(plan_ref, pairs_ref, *refs):
    held, keep_ref, send_ref, unpacked, acc = refs[:-4], *refs[-4:]
    clusters = keep_ref.shape[0]
    quarter = held[0].shape[0]
    rank = pairs_ref.shape[1]
    mask = (1 << FIELD) - 1
    for d, packed in enumerate(held):
        unpacked[2 * d * quarter : (2 * d + 1) * quarter] = packed[:, :, :rank]
        unpacked[(2 * d + 1) * quarter : (2 * d + 2) * quarter] = packed[:, :, rank:]
    acc[...] = jnp.zeros_like(acc)

    def step(i, carry):
        words = [plan_ref[0, i * FAR_UNROLL + j] for j in range(FAR_UNROLL)]
        terms = []
        for j, word in enumerate(words):
            terms.append(dot(unpacked[word & mask], pairs_ref[i * FAR_UNROLL + j], TRANSPOSED_RHS))
        for word, term in zip(words, terms):
            row = lax.shift_right_logical(word, FIELD) & mask
            acc[row] = acc[row] + term
        return carry

    lax.fori_loop(0, lax.div(plan_ref[2, 0] + FAR_UNROLL - 1, FAR_UNROLL), step, 0)
    half = clusters // 2
    for n in range(half):
        keep_ref[n] = acc[n]
        keep_ref[n + half] = acc[n + half]
        send_ref[n] = jnp.concatenate([acc[n], acc[n + half]], 1).astype(jnp.bfloat16)


def finish_kernel(plan_ref, same_ref, other_ref, blocks_ref, acc_in, far_ref, far_other_ref, basis_ref, *refs):
    out_hbm, (acc_ref, whole, out_ref, sent) = refs[0], refs[-4:]
    near_halves_kernel(2, plan_ref, same_ref, other_ref, blocks_ref, acc_in, acc_ref, whole)
    half, _, wide = far_other_ref.shape
    rank = wide // 2
    pieces = sent.shape[0]
    size = 2 * half // pieces
    copies = []
    for n in range(2 * half):
        other = far_other_ref[n, :, :rank] if n < half else far_other_ref[n - half, :, rank:]
        far_low = (far_ref[n] + other.astype(jnp.float32)).astype(jnp.bfloat16)
        out_ref[n] = acc_ref[n] + dot(far_low, basis_ref[n], PLAIN)
        if (n + 1) % size == 0:
            rows = pl.ds(n + 1 - size, size)
            copies.append(pltpu.make_async_copy(out_ref.at[rows], out_hbm.at[rows], sent.at[n // size]))
            copies[-1].start()
    if len(refs) == 9:
        mine_ref, keep_ref, send_ref, parts = refs[1:5]
        low = out_ref[...].astype(jnp.bfloat16)
        mine_ref[...] = low
        send_ref[: 2 * half] = low
        put_projection(mine_ref, basis_ref, keep_ref, send_ref, 2 * half, parts)
    for copy in copies:
        copy.wait()


def tiled_on_device(right_panel, near_field_blocks, near_list, cluster_basis, coupling, far_list):
    clusters, points, columns = right_panel.shape
    near_count = near_list.shape[0]
    slab, rank = cluster_basis.shape[1:]
    panel = right_panel.transpose(0, 2, 1)
    basis = cluster_basis.transpose(0, 2, 1)
    cycle = lax.axis_size("blk")
    half, quarter = clusters // 2, clusters // 4
    f32, bf16 = jnp.float32, jnp.bfloat16
    mine_shape = jax.ShapeDtypeStruct((clusters, columns, slab), bf16)
    keep_shape = jax.ShapeDtypeStruct((quarter, columns, 2 * rank), f32)
    send_shape = jax.ShapeDtypeStruct((quarter, columns, 2 * rank), bf16)
    both_shape = jax.ShapeDtypeStruct((clusters + quarter, columns, slab), bf16)
    parts = pltpu.VMEM((2, quarter, columns, 2 * rank), f32)
    out_shape = jax.ShapeDtypeStruct((clusters, columns, slab), f32)
    acc_shape = jax.ShapeDtypeStruct((clusters + 1, columns, slab), f32)
    near_plan_shape = jax.ShapeDtypeStruct((4, near_count + UNROLL), jnp.int32)
    far_plan_shape = jax.ShapeDtypeStruct((3, far_list.shape[0] + FAR_UNROLL), jnp.int32)

    low_shape = jax.ShapeDtypeStruct((clusters, columns, points), bf16)
    pieces = 4
    mine, basis, keep, send = pl.pallas_call(
        start_kernel,
        out_shape=(mine_shape, jax.ShapeDtypeStruct(basis.shape, bf16), keep_shape, send_shape),
        in_specs=[HBM, HBM],
        out_specs=(VMEM,) * 4,
        scratch_shapes=[pltpu.VMEM(mine_shape.shape, f32), parts, pltpu.SemaphoreType.DMA((2 * pieces,))],
        compiler_params=params(),
        cost_estimate=cost(2),
        name="start",
    )(in_hbm(panel), in_hbm(basis))
    near_plan, far_plan, blocks, pairs = pl.pallas_call(
        functools.partial(prepare_kernel, clusters),
        out_shape=(
            pltpu.SMEM(near_plan_shape.shape, jnp.int32),
            pltpu.SMEM(far_plan_shape.shape, jnp.int32),
            pltpu.VMEM(near_field_blocks.shape, bf16),
            pltpu.VMEM((coupling.shape[0] + FAR_UNROLL, rank, rank), bf16),
        ),
        in_specs=[HBM] * 4,
        out_specs=(SMEM, SMEM, VMEM, VMEM),
        scratch_shapes=[
            pltpu.VMEM((rank, rank, coupling.shape[0]), bf16),
            pltpu.VMEM(((rank + 1) * coupling.shape[0], rank), f32),
            pltpu.VMEM(near_plan_shape.shape, jnp.int32),
            pltpu.VMEM(far_plan_shape.shape, jnp.int32),
            pltpu.VMEM((2, 2, near_count), jnp.int32),
            pltpu.SemaphoreType.DMA((16,)),
        ],
        compiler_params=params(20),
        cost_estimate=cost(4),
        name="prepare",
    )(*(in_hbm(array) for array in (near_list.T, far_list.T, near_field_blocks, coupling.transpose(1, 2, 0))))

    def near_own(plan, blocks):
        return pl.pallas_call(
            near_own_kernel,
            out_shape=acc_shape,
            in_specs=[SMEM, HBM, VMEM],
            out_specs=VMEM,
            scratch_shapes=[
                pltpu.VMEM(panel.shape, f32),
                pltpu.VMEM(low_shape.shape, bf16),
                pltpu.SemaphoreType.DMA,
            ],
            compiler_params=params(),
            cost_estimate=cost(3),
            name="near_own",
        )(in_smem(plan), panel, blocks)

    def near_halves(plan, blocks, kind, same, other, *acc):
        return pl.pallas_call(
            functools.partial(near_halves_kernel, kind),
            out_shape=acc_shape,
            in_specs=[SMEM] + [VMEM] * (3 + len(acc)),
            out_specs=VMEM,
            scratch_shapes=[pltpu.VMEM(low_shape.shape, bf16)],
            compiler_params=params(),
            cost_estimate=cost(2),
            name="near_halves",
        )(in_smem(plan), same, other, blocks, *acc)

    def far(plan, held):
        return pl.pallas_call(
            far_kernel,
            out_shape=(
                jax.ShapeDtypeStruct((clusters, columns, rank), f32),
                jax.ShapeDtypeStruct((half, columns, 2 * rank), bf16),
            ),
            in_specs=[SMEM, VMEM] + [VMEM] * len(held),
            out_specs=(VMEM, VMEM),
            scratch_shapes=[
                pltpu.VMEM((cycle * half, columns, rank), bf16),
                pltpu.VMEM((clusters + 1, columns, rank), f32),
            ],
            compiler_params=params(),
            cost_estimate=cost(3),
            name="far",
        )(in_smem(plan), pairs, *held)

    def finish(plan, blocks, same, other, acc, far_sum, far_other, last):
        outs = (out_shape,) if last else (out_shape, mine_shape, keep_shape, both_shape)
        return pl.pallas_call(
            finish_kernel,
            out_shape=outs,
            in_specs=[SMEM] + [VMEM] * 7,
            out_specs=(HBM,) + (VMEM,) * (len(outs) - 1),
            scratch_shapes=([] if last else [parts])
            + [pltpu.VMEM(acc_shape.shape, f32), pltpu.VMEM(low_shape.shape, bf16)]
            + [pltpu.VMEM(out_shape.shape, f32), pltpu.SemaphoreType.DMA((4,))],
            compiler_params=params(),
            cost_estimate=cost(4),
            name="finish",
        )(in_smem(plan), same, other, blocks, acc, far_sum, far_other, basis)

    def other_basis(array):
        return swapped(array, "basis", lambda i: 1 - i)

    def apply_operator(mine, keep, send, near_plan, last):
        crossing = swapped(mine, "blk", lambda i: (((i + 1) % cycle ^ 1) - 1) % cycle)
        paired = swapped(mine, "blk", lambda i: i ^ 1)
        received = other_basis(send)
        if last:
            acc = near_halves(near_plan, blocks, 0, mine, received)
        else:
            acc = near_own(near_plan, blocks)
        held = [(keep + received[-quarter:].astype(f32)).astype(bf16)]
        got = {0: held[0]}
        for d in reversed([1 << i for i in range(cycle.bit_length() - 1)]):
            for e in list(got):
                got[e ^ d] = swapped(got[e], "blk", lambda i, d=d: i ^ d)
        held = [got[d] for d in range(cycle)]
        if last:
            paired, acc, held[1], held[2] = lax.optimization_barrier((paired, acc, held[1], held[2]))
        else:
            paired, acc, held[2] = lax.optimization_barrier((paired, acc, held[2]))
        crossing_other = other_basis(crossing)
        paired_other = other_basis(paired)
        far_sum, far_send = far(far_plan, held)
        far_other = other_basis(far_send)
        acc = near_halves(near_plan, blocks, 1, crossing, crossing_other, acc)
        return finish(near_plan, blocks, paired, paired_other, acc, far_sum, far_other, last), near_plan

    (first, mine, keep, send), near_plan = apply_operator(mine, keep, send, near_plan, False)
    (second,), _ = apply_operator(mine, keep, send, near_plan, True)
    return first.transpose(0, 2, 1), second.transpose(0, 2, 1)


def from_behind(array, axis, by):
    size = lax.axis_size(axis)
    return lax.ppermute(array, axis, [(i, (i + by) % size) for i in range(size)])


def general_on_device(right_panel, near_field_blocks, near_list, cluster_basis, coupling, far_list):
    highest_precision = lax.Precision.HIGHEST
    clusters = right_panel.shape[0]
    slab_rows = cluster_basis.shape[1]
    cycle_place = lax.axis_index("blk")
    cycle_size = lax.axis_size("blk")
    basis_owner = lax.axis_index("basis")
    cluster_ids = jnp.arange(clusters, dtype=jnp.int32)
    near_rows = near_list[:, 0] - cycle_place * clusters
    near_cols = near_list[:, 1]
    row_lookup_table = (near_rows[None, :] == cluster_ids[:, None]).astype(jnp.float32)
    far_table = ((far_list[:, 0] - cycle_place * clusters)[None, :] == cluster_ids[:, None]).astype(
        jnp.float32
    )
    slot_index = (
        near_cols // clusters - cycle_place + 1 + cycle_size
    ) % cycle_size * clusters + near_cols % clusters

    def apply_operator(panel_low):
        own_rows = lax.dynamic_slice_in_dim(panel_low, basis_owner * slab_rows, slab_rows, 1)
        partial_sum = jnp.einsum(
            "nrk,nrc->nkc", cluster_basis, own_rows, preferred_element_type=jnp.float32
        )
        projected = lax.psum(partial_sum, "basis").astype(jnp.bfloat16)
        projections_all = lax.all_gather(projected, "blk", axis=0, tiled=True)
        far_terms = jnp.einsum(
            "pkr,prc->pkc",
            coupling,
            projections_all[far_list[:, 1]],
            preferred_element_type=jnp.float32,
        )
        far_sum = jnp.einsum("np,pkc->nkc", far_table, far_terms, precision=highest_precision)
        far_low = far_sum.astype(jnp.bfloat16)
        pieces = []
        for offset in (1, -1):
            pieces.append(from_behind(panel_low, "blk", offset))
        window = jnp.concatenate([pieces[0], panel_low, pieces[1]], 0)
        source_vector = window[slot_index]
        near_field_products = jnp.einsum(
            "fpz,fzg->fpg", near_field_blocks, source_vector, preferred_element_type=jnp.float32
        )
        near_field_total = jnp.einsum(
            "id,dpb->ipb", row_lookup_table, near_field_products, precision=highest_precision
        )
        far_part = jnp.einsum(
            "nrk,nkc->nrc", cluster_basis, far_low, preferred_element_type=jnp.float32
        )
        return far_part + near_field_total

    krylov_one = apply_operator(right_panel.astype(jnp.bfloat16))
    second_low = lax.all_gather(krylov_one.astype(jnp.bfloat16), "basis", axis=1, tiled=True)
    krylov_two = apply_operator(second_low)
    return (krylov_one, krylov_two)


def on_device(right_panel, near_field_blocks, near_list, cluster_basis, coupling, far_list):
    cycle = lax.axis_size("blk")
    tiled = lax.axis_size("basis") == 2 and cluster_basis.shape[1] % 128 == 0
    tiled = tiled and cycle >= 4 and cycle & (cycle - 1) == 0
    clusters = right_panel.shape[0]
    tiled = tiled and clusters & (clusters - 1) == 0
    run = tiled_on_device if tiled else general_on_device
    return run(right_panel, near_field_blocks, near_list, cluster_basis, coupling, far_list)


def solution(mesh):
    placed = (
        P(("groups", "blk"), None, "col"),
        P(("groups", "blk"), "basis", None),
        P(("groups", "blk"), None),
        P(("groups", "blk"), "basis", None),
        P(("groups", "blk"), None, None),
        P(("groups", "blk"), None),
    )
    return jax.shard_map(
        on_device,
        mesh=mesh,
        in_specs=placed,
        out_specs=(P(("groups", "blk"), "basis", "col"), P(("groups", "blk"), "basis", "col")),
        check_vma=False,
    )
```
